32 devices in a mesh: segment: 2 (over x), owner: 16 (over z, y, core).
Axes of the slice: x: 2, y: 2, z: 4, core: 2. Of those that a mesh axis runs over, the one named last changes fastest.
Arguments:
- layer_input_rows: bfloat16 [2, 2048, 4096], P('segment', 'owner'), may hold values from -6 to 6
- output_gradient: bfloat16 [2, 2048, 1024], P('segment', 'owner'), may hold values from -6 to 6
- tenant: int32 [2048, 1], P('owner'), may hold values from 0 to 15; in each aligned block of 128 rows (0 to 127, 128 to 255, ...) at most 16 rows name the same one
- adapter_owner_index: int32 [16], replicated, may hold values from 0 to 15, each once
- adapter_down_weight: bfloat16 [2, 16, 4096, 64], P('segment', 'owner'), may hold values from -0.09375 to 0.09375
- adapter_up_weight: bfloat16 [2, 16, 64, 1024], P('segment', 'owner'), may hold values from -0.1875 to 0.1875
Outputs:
- passed_grad: bfloat16 [2, 2048, 4096], P('segment', 'owner')
- grad_down: float32 [2, 16, 4096, 64], P('segment', 'owner')
- grad_up: float32 [2, 16, 64, 1024], P('segment', 'owner')
The draws below stay inside these ranges and needn't reach their ends.
Inputs may be any that keep to these rules, and one draw needn't show every extreme that they name: `tenant`: within the rows of one device no adapter is named by more than 16 rows, and in every draw some device names some adapter exactly 16 times. `adapter_owner_index`: each owner index appears once.
All inputs are finite; a program needn't handle non-finite values.
Results may differ from the reference program's by a relative error of at most 0.014.
Values may be sent and summed in bfloat16 or wider, within the bound.
A program may use at most 128 MiB of HBM per device.

```python
import math
import jax
import jax.numpy as jnp
import numpy as np
from jax import lax

MODEL_WIDTH = 4096
VALUE_WIDTH = 1024
ADAPTER_RANK = 64
TOK_DEV = 128
ROW_LIMIT = 16
ADAPTERS = 16
TOKENS = 2048
N_SEGMENT = 2
N_OWNER = 16


def block_scale(key, shape, shards, least, top_value):
    loudness, own = 1.0, jax.random.fold_in(key, 6)
    for position, parts in shards:
        heights = jnp.exp(jax.random.uniform(jax.random.fold_in(own, position), (parts,), jnp.float32, least / len(shards), top_value / len(shards)))
        loudness = loudness * jnp.repeat(heights, shape[position] // parts).reshape([-1 if axis == position else 1 for axis in range(len(shape))])
    return loudness


def deal_out(stream_key, own, number, rows, amount, top, reach, skew):
    order = jax.random.permutation(stream_key, amount)
    heavy_load, common = portions_of(amount, rows * top, reach, skew, True), portions_of(amount, rows * top, reach, skew, False)
    places = jnp.arange(amount)

    def named(sizes, turn):
        used = int((sizes > 0).sum())
        fixed = max(1, used // 4)
        shifted = fixed + (places - fixed + turn * (used - fixed)) % max(1, amount - fixed)
        return jnp.zeros((amount,), jnp.int32).at[order[jnp.where(places < fixed, places, shifted)]].set(jnp.asarray(sizes, jnp.int32))

    sizes = jnp.where(number % 4 == 0, named(heavy_load, number // 4), named(common, number - number // 4 - 1))
    mixed = jax.random.permutation(jax.random.fold_in(own, 3), amount)
    source_of, sink = mixed[0:amount // 2 * 2:2], mixed[1:amount // 2 * 2:2]
    slack = jnp.minimum(sizes[source_of] - 1, reach - sizes[sink]) // 2
    slack = jnp.where((source_of == order[0]) | (sink == order[0]) | (sizes[sink] == 0), 0, jnp.maximum(slack, 0))
    shifted = jax.random.randint(jax.random.fold_in(own, 4), (amount // 2,), 0, 1 << 20) % (slack + 1)
    sizes = sizes.at[source_of].add(-shifted).at[sink].add(shifted)
    members = jnp.searchsorted(jnp.cumsum(sizes), jnp.arange(rows * top), side="right").astype(jnp.int32)
    grid = members.reshape(top, rows).T
    grid = grid[jax.random.permutation(jax.random.fold_in(own, 1), rows)]
    turn = jax.random.randint(jax.random.fold_in(own, 2), (rows, 1), 0, top)
    return jnp.take_along_axis(grid, (jnp.arange(top)[None, :] + turn) % top, axis=1)


def portions_of(amount, total, bound, lean, full):
    portions = [(1 << 20) // math.isqrt(grade ** lean) + 1 for grade in range(1, amount + 1)]
    largest = bound if full else min(bound, max(-(-total // amount), total * portions[0] // sum(portions)))
    least = 1 if total - largest >= amount - 1 else 0
    given, surplus = [largest] + [least] * (amount - 1), total - largest - least * (amount - 1)
    while surplus > 0:
        candidates = [i for i in range(1, amount) if given[i] < largest] or [i for i in range(1, amount) if given[i] < bound]
        pool, remaining = sum([portions[i] for i in candidates]), surplus
        for i in candidates:
            more = min(bound - given[i], max(1, remaining * portions[i] // pool), surplus)
            given[i] = given[i] + more
            surplus = surplus - more
    return np.array(given)


def noise(own_key, dims, width, bound, split=(), kind=jnp.bfloat16):
    entries = jax.random.normal(own_key, dims, jnp.float32) * width
    if len(split) > 0:
        entries = block_scale(own_key, dims, split, -0.22, 0.18) * entries
    return jnp.clip(entries, min=-bound, max=bound).astype(kind)


def setup_inputs(seed: int = 0) -> dict:
    arg_keys = jax.random.split(jax.random.key(seed), 7)
    layer_input_rows = noise(arg_keys[0], (N_SEGMENT, TOKENS, MODEL_WIDTH), 1.0, 6.0, ((0, 2), (1, 16)))
    output_gradient = noise(arg_keys[1], (N_SEGMENT, TOKENS, VALUE_WIDTH), 1.0, 6.0, ((0, 2), (1, 16)))
    tenant_keys = jax.random.split(jax.random.fold_in(arg_keys[2], 1), TOKENS // TOK_DEV)
    tenant_turns = jax.random.permutation(jax.random.fold_in(arg_keys[2], 3), TOKENS // TOK_DEV)
    tenant = jax.vmap(lambda own, number: deal_out(jax.random.fold_in(arg_keys[2], 2), own, number, TOK_DEV, ADAPTERS, 1, ROW_LIMIT, 2))(tenant_keys, tenant_turns).reshape((TOKENS, 1))
    adapter_owner_index = jax.random.permutation(arg_keys[3], ADAPTERS).astype(jnp.int32)
    adapter_down_weight = noise(arg_keys[4], (N_SEGMENT, N_OWNER, MODEL_WIDTH, ADAPTER_RANK), MODEL_WIDTH ** -0.5, 0.09375, ((0, 2), (1, 16)))
    adapter_up_weight = noise(arg_keys[5], (N_SEGMENT, N_OWNER, ADAPTER_RANK, VALUE_WIDTH), VALUE_WIDTH ** -0.5, 0.1875, ((0, 2), (1, 16)))
    return {"layer_input_rows": layer_input_rows, "output_gradient": output_gradient, "tenant": tenant, "adapter_owner_index": adapter_owner_index, "adapter_down_weight": adapter_down_weight, "adapter_up_weight": adapter_up_weight}


adapter_scale = 2.0


def reference(layer_input_rows, output_gradient, tenant, adapter_owner_index, adapter_down_weight, adapter_up_weight):
    ids = tenant[:, 0].astype(jnp.int32)
    dest = adapter_owner_index[ids].astype(jnp.int32)
    source = jnp.arange(TOKENS, dtype=jnp.int32) // TOK_DEV
    onehot = (dest[:, None] == jnp.arange(N_OWNER, dtype=jnp.int32)[None, :]).astype(jnp.int32)
    onehot = onehot.reshape(N_OWNER, TOK_DEV, N_OWNER)
    ranked = (jnp.cumsum(onehot, axis=1) - 1) * onehot
    rank = jnp.sum(ranked, axis=2).reshape(TOKENS).astype(jnp.int32)
    location_mask = dest * (N_OWNER * ROW_LIMIT) + source * ROW_LIMIT + rank
    row_count_total = N_OWNER * N_OWNER * ROW_LIMIT
    highest_precision = lax.Precision.HIGHEST

    def single_section(items):
        inputs, gradient_list, down_factor, up_factor = items
        xbuf = jnp.zeros((row_count_total, MODEL_WIDTH), jnp.float32).at[location_mask].set(inputs.astype(jnp.float32))
        xbuf = xbuf.reshape(N_OWNER, N_OWNER * ROW_LIMIT, MODEL_WIDTH)
        gradient_buffer = jnp.zeros((row_count_total, VALUE_WIDTH), jnp.float32).at[location_mask].set(gradient_list.astype(jnp.float32))
        gradient_buffer = gradient_buffer.reshape(N_OWNER, N_OWNER * ROW_LIMIT, VALUE_WIDTH)
        down32 = down_factor.astype(jnp.float32)
        up_factor_float32 = up_factor.astype(jnp.float32)
        scale_weight = adapter_scale * jnp.einsum('lgd,lwd->lgw', gradient_buffer, up_factor_float32, precision=highest_precision)
        projected_rows = jnp.einsum('ord,odk->ork', xbuf, down32, precision=highest_precision)
        down_gradient = jnp.einsum('ord,ork->odk', xbuf, scale_weight, precision=highest_precision)
        up_gradient = jnp.einsum('gbl,gbw->glw', projected_rows, gradient_buffer, precision=highest_precision)
        term = jnp.einsum('ork,odk->ord', scale_weight, down32, precision=highest_precision).astype(jnp.bfloat16)
        term = term.reshape(row_count_total, MODEL_WIDTH)[location_mask]
        return term, down_gradient, up_gradient

    partial_terms, down_gradient, up_gradient = lax.map(single_section, (layer_input_rows, output_gradient, adapter_down_weight, adapter_up_weight))
    suffix = jnp.flip(jnp.cumsum(jnp.flip(partial_terms.astype(jnp.float32), 0), 0), 0)
    return suffix.astype(jnp.bfloat16), down_gradient, up_gradient
```

```python
import functools

import jax
import jax.numpy as jnp
from jax import lax
from jax.experimental import pallas as pl
from jax.experimental.pallas import tpu as pltpu
from jax.sharding import PartitionSpec as P

adapter_scale = 2.0


def prefix(x, axis, join, neutral):
    count = lax.axis_size(axis)
    place = lax.axis_index(axis)
    ahead = count - 1 - place
    gathered = lax.all_gather(x.astype(jnp.bfloat16), axis)
    state = jnp.zeros_like(x) + jnp.asarray(neutral, x.dtype)

    def one(step, state):
        source = count - 1 - step
        return join(state, lax.dynamic_index_in_dim(gathered, source, 0, False).astype(x.dtype))

    return lax.fori_loop(0, ahead, one, state)


def local(
    layer_input_rows,
    output_gradient,
    tenant,
    adapter_owner_index,
    adapter_down_weight,
    adapter_up_weight,
):
    inputs = layer_input_rows[0]
    gradient_list = output_gradient[0]
    tok_rows = inputs.shape[0]
    width = inputs.shape[1]
    out_width = gradient_list.shape[1]
    owners = lax.axis_size("owner")
    capacity = 2 * tok_rows // owners
    highest_precision = lax.Precision.HIGHEST
    ids = tenant[:, 0]
    adapter_count = adapter_owner_index.shape[0]
    matched = ids[:, None] == jnp.arange(adapter_count, dtype=jnp.int32)[None, :]
    dest = jnp.sum(jnp.where(matched, adapter_owner_index[None, :], 0), axis=1)
    onehot = (dest[:, None] == jnp.arange(owners, dtype=jnp.int32)[None, :]).astype(jnp.int32)
    rank = jnp.sum((jnp.cumsum(onehot, axis=0) - 1) * onehot, axis=1)
    target = dest * capacity + rank
    placing = (jnp.arange(owners * capacity, dtype=jnp.int32)[:, None] == target[None, :]).astype(
        jnp.bfloat16
    )
    send_inputs = jnp.dot(placing, inputs, preferred_element_type=jnp.float32).astype(jnp.bfloat16)
    send_grads = jnp.dot(placing, gradient_list, preferred_element_type=jnp.float32).astype(
        jnp.bfloat16
    )
    send_inputs = send_inputs.reshape(owners, capacity, width)
    send_grads = send_grads.reshape(owners, capacity, out_width)
    down_factor = adapter_down_weight[0, 0]
    up_factor = adapter_up_weight[0, 0]
    recv_inputs, recv_grads = (
        lax.all_to_all(send_inputs, "owner", split_axis=0, concat_axis=0, tiled=True),
        lax.all_to_all(send_grads, "owner", split_axis=0, concat_axis=0, tiled=True),
    )
    rows_in = recv_inputs.reshape(owners * capacity, width)
    rows_grad = recv_grads.reshape(owners * capacity, out_width)
    scale_weight = adapter_scale * jnp.einsum(
        "rm,km->rk", rows_grad, up_factor, preferred_element_type=jnp.float32
    )
    partial_terms = jnp.einsum(
        "rk,dk->rd",
        scale_weight,
        down_factor,
        precision=highest_precision,
        preferred_element_type=jnp.float32,
    )
    partial_terms = partial_terms.astype(jnp.bfloat16).reshape(owners, capacity, width)
    returned = lax.all_to_all(partial_terms, "owner", split_axis=0, concat_axis=0, tiled=True)
    projected_rows = jnp.dot(rows_in, down_factor, preferred_element_type=jnp.float32)
    grad_down = jnp.einsum(
        "rd,rk->dk",
        rows_in,
        scale_weight,
        precision=highest_precision,
        preferred_element_type=jnp.float32,
    )
    grad_up = jnp.einsum(
        "rk,rm->km",
        projected_rows,
        rows_grad,
        precision=highest_precision,
        preferred_element_type=jnp.float32,
    )
    own_term = jnp.einsum(
        "sr,sd->rd",
        placing,
        returned.reshape(owners * capacity, width),
        preferred_element_type=jnp.float32,
    )

    def combine(earlier, later):
        return earlier + later

    above = prefix(own_term, "segment", combine, jnp.zeros_like(own_term))
    passed = (above + own_term).astype(jnp.bfloat16)
    return (passed[None], grad_down[None, None], grad_up[None, None])


lines = 4
plane = 4
chunks = 2
bf16 = jnp.bfloat16
f32 = jnp.float32


def dot_nt(a, b):
    return lax.dot_general(a, b, (((1,), (1,)), ((), ())), preferred_element_type=f32)


def dot_nn(a, b):
    return jnp.dot(a, b, preferred_element_type=f32)


def lines_kernel(
    x, g, ids, owner_of, a, b,
    passed, gd, gu,
    sx, sg, rx, rg, at, bt, a1, cf, cft, c1, ts, tr, sl, sr, ql, qr, ul, ur, vl, vr, gup,
    x_s, x_r, g_s, g_r, a_s, a_r, b_s, b_r, a1_s, a1_r, c_s, c_r, t_s, t_r, d_s, d_r, u_s, u_r,
):
    tok, width = x.shape
    out_width = g.shape[1]
    part = width // chunks
    cap = sx.shape[3]
    rank_dim = b.shape[0]
    rows = plane * cap
    seg = lax.axis_index("segment")
    own = lax.axis_index("owner")
    z = own // plane
    h = own % plane
    upper = seg == 1
    lower = seg == 0
    pending = []

    def signal(segment, owner):
        pl.semaphore_signal(
            barrier, inc=1, device_id=(segment, owner), device_id_type=pl.DeviceIdType.MESH
        )

    def copy(source, sink, send, recv, segment, owner):
        return pltpu.make_async_remote_copy(
            src_ref=source, dst_ref=sink, send_sem=send, recv_sem=recv,
            device_id=(segment, owner), device_id_type=pl.DeviceIdType.MESH,
        )

    def go(cond, make):
        if cond is None:
            make().start()
        else:
            pl.when(cond)(lambda: make().start())
        pending.append((cond, make))

    def host(k):
        return z * plane + (h + k) % plane

    has_left = z > 0
    has_right = z < lines - 1

    barrier = pltpu.get_barrier_semaphore()
    for k in range(1, plane):
        signal(seg, host(k))
    signal(1 - seg, own)
    pl.when(has_left)(lambda: signal(seg, own - plane))
    pl.when(has_right)(lambda: signal(seg, own + plane))

    n_owner = lines * plane
    n_adapter = owner_of.shape[0]
    matched = lax.broadcasted_iota(jnp.int32, (n_adapter, tok), 0) == ids[...]
    dest = jnp.sum(jnp.where(matched, owner_of[...], 0), axis=0, keepdims=True)
    onehot = (lax.broadcasted_iota(jnp.int32, (n_owner, tok), 0) == dest).astype(f32)
    earlier = (
        lax.broadcasted_iota(jnp.int32, (tok, tok), 0)
        < lax.broadcasted_iota(jnp.int32, (tok, tok), 1)
    ).astype(f32)
    count = dot_nn(onehot.astype(bf16), earlier.astype(bf16))
    rank = jnp.sum(count * onehot, axis=0, keepdims=True).astype(jnp.int32)
    target = (dest % plane) * (lines * cap) + (dest // plane) * cap + rank
    placing32 = (
        lax.broadcasted_iota(jnp.int32, (plane * lines * cap, tok), 0) == target
    ).astype(f32)
    placing = placing32.astype(bf16)
    placing_t = placing32.T.astype(bf16)

    at[z] = a[...]
    bt[z] = b[...]
    sg[...] = dot_nn(placing, g[...]).astype(bf16).reshape(plane, lines, cap, out_width)
    pl.semaphore_wait(
        barrier, plane + jnp.where(has_left, 1, 0) + jnp.where(has_right, 1, 0)
    )

    def shard_go(buf, send, recv, k):
        go(
            (z >= k) & has_right,
            lambda: copy(buf.at[z - k], buf.at[z - k], send.at[0, k], recv.at[z - k], seg, own + plane),
        )
        go(
            (z + k < lines) & has_left,
            lambda: copy(buf.at[z + k], buf.at[z + k], send.at[1, k], recv.at[z + k], seg, own - plane),
        )

    def shard_wait(buf, send, recv, k):
        pl.when(z >= k)(
            lambda: copy(buf.at[z - k], buf.at[z - k], send.at[0, k], recv.at[z - k], seg, host(1)).wait_recv()
        )
        pl.when(z + k < lines)(
            lambda: copy(buf.at[z + k], buf.at[z + k], send.at[1, k], recv.at[z + k], seg, host(1)).wait_recv()
        )

    def across(j):
        return copy(at.at[j], a1.at[j], a1_s.at[j], a1_r.at[j], 0, own)

    def a_step(k):
        shard_wait(at, a_s, a_r, k)
        if k < lines - 1:
            shard_go(at, a_s, a_r, k)
        go((z >= k) & upper, lambda: across(z - k))
        go((z + k < lines) & upper, lambda: across(z + k))

    def g_copy(k):
        return copy(
            sg.at[(h + k) % plane], rg.at[:, h], g_s.at[k - 1], g_r.at[k - 1], seg, host(k)
        )

    def x_copy(q, k):
        return copy(
            sx.at[q, (h + k) % plane], rx.at[q, :, h], x_s.at[q, k - 1], x_r.at[q, k - 1], seg, host(k)
        )

    shard_go(bt, b_s, b_r, 0)
    for k in range(1, plane):
        go(None, functools.partial(g_copy, k))
    shard_go(at, a_s, a_r, 0)
    go(upper, lambda: across(z))
    rg[:, h] = sg[h]
    for q in range(chunks):
        sx[q] = (
            dot_nn(placing, x[:, q * part : (q + 1) * part])
            .astype(bf16)
            .reshape(plane, lines, cap, part)
        )
        for k in range(1, plane):
            go(None, functools.partial(x_copy, q, k))
        rx[q, :, h] = sx[q, h]
    for k in range(1, lines):
        shard_wait(bt, b_s, b_r, k)
        if k < lines - 1:
            shard_go(bt, b_s, b_r, k)

    cf[...] = jnp.zeros_like(cf)
    for k in range(1, plane):
        g_copy(k).wait_recv()
    for j in range(lines):
        grads = rg[j].reshape(rows, out_width)
        cf[j, :, :rank_dim] = (adapter_scale * dot_nt(grads, bt[j])).astype(bf16)
        cft[j, :, :rows] = (adapter_scale * dot_nt(bt[j], grads)).astype(bf16)

    def coef_copy():
        return copy(cf, c1, c_s, c_r, 0, own)

    go(upper, coef_copy)
    a_step(1)

    def sums(value, cols, send_l, send_r, recv_l, recv_r, s_sem, r_sem):
        def left(t):
            return copy(send_l.at[t], recv_l.at[t], s_sem.at[0, t], r_sem.at[0, t], seg, own - plane)

        def right(t):
            return copy(send_r.at[t], recv_r.at[t], s_sem.at[1, t], r_sem.at[1, t], seg, own + plane)

        for t in range(lines - 1):
            for goal, buf, got, make, cond, more in (
                (t, send_l, recv_l, left, z > t, has_right),
                (lines - 1 - t, send_r, recv_r, right, z < lines - 1 - t, has_left),
            ):
                @pl.when(cond & jnp.logical_not(more))
                def _():
                    buf[goal] = value(goal).astype(bf16)

                @pl.when(cond & more)
                def _():
                    mine = value(goal)
                    make(goal).wait_recv()
                    buf[goal] = (mine + got[goal].astype(f32)).astype(bf16)

                go(cond, functools.partial(make, goal))

        def finish(out):
            out[:, cols] = value(z)

            @pl.when(has_right)
            def _():
                left(z).wait_recv()
                out[:, cols] += recv_l[z].astype(f32)

            @pl.when(has_left)
            def _():
                right(z).wait_recv()
                out[:, cols] += recv_r[z].astype(f32)

        return finish

    def down_sums(q):
        for k in range(1, plane):
            x_copy(q, k).wait_recv()
        return sums(
            lambda j: dot_nn(cft[j, :, :rows], rx[q, j].reshape(rows, part)),
            pl.ds(q * part, part),
            sl.at[q], sr.at[q], ql.at[q], qr.at[q], d_s.at[q], d_r.at[q],
        )

    order = (z, z + 1 - 2 * (z % 2), 2 - z // 2, 3 - 3 * (z // 2))

    def t_copy(i, k):
        return copy(
            ts.at[order[i], (h + k) % plane], tr.at[h, order[i]],
            t_s.at[i, k - 1], t_r.at[i, k - 1], seg, host(k),
        )

    def term(i):
        j = order[i]
        for q in range(chunks):
            cols = pl.ds(q * part, part)
            mine = dot_nn(cf[j, :, :rank_dim], at[j, :, cols]).astype(bf16)

            @pl.when(upper)
            def _():
                ts[j, :, :, cols] = mine.reshape(plane, cap, part)

            @pl.when(lower)
            def _():
                if q == 0:
                    across(j).wait_recv()
                above = dot_nn(c1[j, :, :rank_dim], a1[j, :, cols]).astype(bf16)
                total = (mine.astype(f32) + above.astype(f32)).astype(bf16)
                ts[j, :, :, cols] = total.reshape(plane, cap, part)

        for k in range(1, plane):
            go(None, functools.partial(t_copy, i, k))
        tr[h, j] = ts[j, h]

    def project(i):
        j = order[i]
        proj = jnp.zeros((rank_dim, rows), f32)
        for q in range(chunks):
            proj += dot_nt(at[j, :, q * part : (q + 1) * part], rx[q, j].reshape(rows, part))
        gup[j] = dot_nn(proj.astype(bf16), rg[j].reshape(rows, out_width))

    ends = [down_sums(0)]
    pl.when(lower)(lambda: coef_copy().wait_recv())
    term(0)
    a_step(2)
    ends.append(down_sums(1))
    term(1)
    project(0)
    project(1)
    a_step(3)
    term(2)
    project(2)
    project(3)
    up_end = sums(lambda j: gup[j], pl.ds(0, out_width), ul, ur, vl, vr, u_s, u_r)
    term(3)
    for end in ends:
        end(gd)
    up_end(gu)
    for i in range(lines):
        for k in range(1, plane):
            t_copy(i, k).wait_recv()
    for q in range(chunks):
        cols = pl.ds(q * part, part)
        passed[:, cols] = dot_nn(
            placing_t, tr[:, :, :, cols].reshape(plane * lines * cap, part)
        ).astype(bf16)
    for cond, make in pending:
        if cond is None:
            make().wait_send()
        else:
            pl.when(cond)(functools.partial(lambda make: make().wait_send(), make))


def local_lines(
    layer_input_rows,
    output_gradient,
    tenant,
    adapter_owner_index,
    adapter_down_weight,
    adapter_up_weight,
):
    x, g = layer_input_rows[0], output_gradient[0]
    tok, width = x.shape
    out_width = g.shape[1]
    rank_dim = adapter_up_weight.shape[2]
    cap = 2 * tok // (lines * plane)
    rows = plane * cap
    part = width // chunks
    lanes = 128
    vmem = pl.BlockSpec(memory_space=pltpu.VMEM)
    dma = pltpu.SemaphoreType.DMA
    passed, gd, gu = pl.pallas_call(
        lines_kernel,
        out_shape=(
            jax.ShapeDtypeStruct((tok, width), bf16),
            jax.ShapeDtypeStruct((rank_dim, width), f32),
            jax.ShapeDtypeStruct((rank_dim, out_width), f32),
        ),
        in_specs=[vmem] * 6,
        out_specs=(vmem,) * 3,
        scratch_shapes=[
            pltpu.VMEM((chunks, plane, lines, cap, part), bf16),
            pltpu.VMEM((plane, lines, cap, out_width), bf16),
            pltpu.VMEM((chunks, lines, plane, cap, part), bf16),
            pltpu.VMEM((lines, plane, cap, out_width), bf16),
            pltpu.VMEM((lines, rank_dim, width), bf16),
            pltpu.VMEM((lines, rank_dim, out_width), bf16),
            pltpu.VMEM((lines, rank_dim, width), bf16),
            pltpu.VMEM((lines, rows, lanes), bf16),
            pltpu.VMEM((lines, rank_dim, lanes), bf16),
            pltpu.VMEM((lines, rows, lanes), bf16),
            pltpu.VMEM((lines, plane, cap, width), bf16),
            pltpu.VMEM((plane, lines, cap, width), bf16),
        ]
        + [pltpu.VMEM((chunks, lines, rank_dim, part), bf16)] * 4
        + [pltpu.VMEM((lines, rank_dim, out_width), bf16)] * 4
        + [
            pltpu.VMEM((lines, rank_dim, out_width), f32),
            dma((chunks, plane - 1)), dma((chunks, plane - 1)),
            dma((plane - 1,)), dma((plane - 1,)),
            dma((2, lines)), dma((lines,)),
            dma((2, lines)), dma((lines,)),
            dma((lines,)), dma((lines,)),
            dma, dma,
            dma((lines, plane - 1)), dma((lines, plane - 1)),
            dma((chunks, 2, lines)), dma((chunks, 2, lines)),
            dma((2, lines)), dma((2, lines)),
        ],
        compiler_params=pltpu.CompilerParams(
            collective_id=0, has_side_effects=True, vmem_limit_bytes=56 * 1024 * 1024
        ),
        name="adapter_lines",
    )(
        x,
        g,
        tenant.reshape(1, tok),
        adapter_owner_index.reshape(-1, 1),
        adapter_down_weight[0, 0].T,
        adapter_up_weight[0, 0],
    )
    return (passed[None], gd.T[None, None], gu[None, None])


def solution(mesh):
    planned = mesh.shape["segment"] == 2 and mesh.shape["owner"] == lines * plane
    return jax.shard_map(
        local_lines if planned else local,
        mesh=mesh,
        in_specs=(
            P("segment", "owner", None),
            P("segment", "owner", None),
            P("owner", None),
            P(),
            P("segment", "owner", None, None),
            P("segment", "owner", None, None),
        ),
        out_specs=(
            P("segment", "owner", None),
            P("segment", "owner", None, None),
            P("segment", "owner", None, None),
        ),
        check_vma=False,
    )
```

```python
import functools

import jax
import jax.numpy as jnp
from jax import lax
from jax.experimental import pallas as pl
from jax.experimental.pallas import tpu as pltpu
from jax.sharding import PartitionSpec as P

adapter_scale = 2.0


def prefix(x, axis, join, neutral):
    count = lax.axis_size(axis)
    place = lax.axis_index(axis)
    ahead = count - 1 - place
    gathered = lax.all_gather(x.astype(jnp.bfloat16), axis)
    state = jnp.zeros_like(x) + jnp.asarray(neutral, x.dtype)

    def one(step, state):
        source = count - 1 - step
        return join(state, lax.dynamic_index_in_dim(gathered, source, 0, False).astype(x.dtype))

    return lax.fori_loop(0, ahead, one, state)


def local(
    layer_input_rows,
    output_gradient,
    tenant,
    adapter_owner_index,
    adapter_down_weight,
    adapter_up_weight,
):
    inputs = layer_input_rows[0]
    gradient_list = output_gradient[0]
    tok_rows = inputs.shape[0]
    width = inputs.shape[1]
    out_width = gradient_list.shape[1]
    owners = lax.axis_size("owner")
    capacity = 2 * tok_rows // owners
    highest_precision = lax.Precision.HIGHEST
    ids = tenant[:, 0]
    adapter_count = adapter_owner_index.shape[0]
    matched = ids[:, None] == jnp.arange(adapter_count, dtype=jnp.int32)[None, :]
    dest = jnp.sum(jnp.where(matched, adapter_owner_index[None, :], 0), axis=1)
    onehot = (dest[:, None] == jnp.arange(owners, dtype=jnp.int32)[None, :]).astype(jnp.int32)
    rank = jnp.sum((jnp.cumsum(onehot, axis=0) - 1) * onehot, axis=1)
    target = dest * capacity + rank
    placing = (jnp.arange(owners * capacity, dtype=jnp.int32)[:, None] == target[None, :]).astype(
        jnp.bfloat16
    )
    send_inputs = jnp.dot(placing, inputs, preferred_element_type=jnp.float32).astype(jnp.bfloat16)
    send_grads = jnp.dot(placing, gradient_list, preferred_element_type=jnp.float32).astype(
        jnp.bfloat16
    )
    send_inputs = send_inputs.reshape(owners, capacity, width)
    send_grads = send_grads.reshape(owners, capacity, out_width)
    down_factor = adapter_down_weight[0, 0]
    up_factor = adapter_up_weight[0, 0]
    recv_inputs, recv_grads = (
        lax.all_to_all(send_inputs, "owner", split_axis=0, concat_axis=0, tiled=True),
        lax.all_to_all(send_grads, "owner", split_axis=0, concat_axis=0, tiled=True),
    )
    rows_in = recv_inputs.reshape(owners * capacity, width)
    rows_grad = recv_grads.reshape(owners * capacity, out_width)
    scale_weight = adapter_scale * jnp.einsum(
        "rm,km->rk", rows_grad, up_factor, preferred_element_type=jnp.float32
    )
    partial_terms = jnp.einsum(
        "rk,dk->rd",
        scale_weight,
        down_factor,
        precision=highest_precision,
        preferred_element_type=jnp.float32,
    )
    partial_terms = partial_terms.astype(jnp.bfloat16).reshape(owners, capacity, width)
    returned = lax.all_to_all(partial_terms, "owner", split_axis=0, concat_axis=0, tiled=True)
    projected_rows = jnp.dot(rows_in, down_factor, preferred_element_type=jnp.float32)
    grad_down = jnp.einsum(
        "rd,rk->dk",
        rows_in,
        scale_weight,
        precision=highest_precision,
        preferred_element_type=jnp.float32,
    )
    grad_up = jnp.einsum(
        "rk,rm->km",
        projected_rows,
        rows_grad,
        precision=highest_precision,
        preferred_element_type=jnp.float32,
    )
    own_term = jnp.einsum(
        "sr,sd->rd",
        placing,
        returned.reshape(owners * capacity, width),
        preferred_element_type=jnp.float32,
    )

    def combine(earlier, later):
        return earlier + later

    above = prefix(own_term, "segment", combine, jnp.zeros_like(own_term))
    passed = (above + own_term).astype(jnp.bfloat16)
    return (passed[None], grad_down[None, None], grad_up[None, None])


lines = 4
plane = 4
chunks = 4
parts = 2
bf16 = jnp.bfloat16
f32 = jnp.float32


def dot_nt(a, b):
    return lax.dot_general(a, b, (((1,), (1,)), ((), ())), preferred_element_type=f32)


def dot_nn(a, b):
    return jnp.dot(a, b, preferred_element_type=f32)


def lines_kernel(
    x, g, ids, owner_of, a, b,
    passed, gd, gu,
    sx, sg, rx, rg, at, bt, a1, cf, cft, c1, ts, tr, sl, sr, ql, qr, ul, ur, vl, vr, gup,
    x_s, x_r, g_s, g_r, a_s, a_r, b_s, b_r, a1_s, a1_r, c_s, c_r, t_s, t_r, d_s, d_r, u_s, u_r,
):
    tok, width = x.shape
    out_width = g.shape[1]
    part = width // chunks
    wide = width // parts
    cap = sx.shape[3]
    rank_dim = b.shape[0]
    rows = plane * cap
    seg = lax.axis_index("segment")
    own = lax.axis_index("owner")
    z = own // plane
    h = own % plane
    upper = seg == 1
    lower = seg == 0
    pending = []

    def signal(segment, owner):
        pl.semaphore_signal(
            barrier, inc=1, device_id=(segment, owner), device_id_type=pl.DeviceIdType.MESH
        )

    def copy(source, sink, send, recv, segment, owner):
        return pltpu.make_async_remote_copy(
            src_ref=source, dst_ref=sink, send_sem=send, recv_sem=recv,
            device_id=(segment, owner), device_id_type=pl.DeviceIdType.MESH,
        )

    def go(cond, make):
        if cond is None:
            make().start()
        else:
            pl.when(cond)(lambda: make().start())
        pending.append((cond, make))

    def host(k):
        return z * plane + (h + k) % plane

    has_left = z > 0
    has_right = z < lines - 1

    barrier = pltpu.get_barrier_semaphore()
    for k in range(1, plane):
        signal(seg, host(k))
    signal(1 - seg, own)
    pl.when(has_left)(lambda: signal(seg, own - plane))
    pl.when(has_right)(lambda: signal(seg, own + plane))

    n_owner = lines * plane
    n_adapter = owner_of.shape[1]
    square = (n_adapter, n_adapter)
    diagonal = lax.broadcasted_iota(jnp.int32, square, 0) == lax.broadcasted_iota(jnp.int32, square, 1)
    owner_column = jnp.sum(jnp.where(diagonal, owner_of[...], 0), axis=1, keepdims=True)
    matched = lax.broadcasted_iota(jnp.int32, (n_adapter, tok), 0) == ids[...]
    dest = jnp.sum(jnp.where(matched, owner_column, 0), axis=0, keepdims=True)
    onehot = (lax.broadcasted_iota(jnp.int32, (n_owner, tok), 0) == dest).astype(f32)
    earlier = (
        lax.broadcasted_iota(jnp.int32, (tok, tok), 0)
        < lax.broadcasted_iota(jnp.int32, (tok, tok), 1)
    ).astype(f32)
    count = dot_nn(onehot.astype(bf16), earlier.astype(bf16))
    rank = jnp.sum(count * onehot, axis=0, keepdims=True).astype(jnp.int32)
    target = (dest % plane) * (lines * cap) + (dest // plane) * cap + rank
    placing32 = (
        lax.broadcasted_iota(jnp.int32, (plane * lines * cap, tok), 0) == target
    ).astype(f32)
    placing = placing32.astype(bf16)
    placing_t = placing32.T.astype(bf16)

    bt[z] = b[...]
    for p in range(parts):
        at[p, z] = a[:, p * wide : (p + 1) * wide]
    sg[...] = dot_nn(placing, g[...]).astype(bf16).reshape(plane, lines, cap, out_width)
    pl.semaphore_wait(
        barrier, plane + jnp.where(has_left, 1, 0) + jnp.where(has_right, 1, 0)
    )

    def shard_go(buf, send, recv, k):
        go(
            (z >= k) & has_right,
            lambda: copy(buf.at[z - k], buf.at[z - k], send.at[0, k], recv.at[z - k], seg, own + plane),
        )
        go(
            (z + k < lines) & has_left,
            lambda: copy(buf.at[z + k], buf.at[z + k], send.at[1, k], recv.at[z + k], seg, own - plane),
        )

    def shard_wait(buf, send, recv, k):
        pl.when(z >= k)(
            lambda: copy(buf.at[z - k], buf.at[z - k], send.at[0, k], recv.at[z - k], seg, host(1)).wait_recv()
        )
        pl.when(z + k < lines)(
            lambda: copy(buf.at[z + k], buf.at[z + k], send.at[1, k], recv.at[z + k], seg, host(1)).wait_recv()
        )

    def across(p, j):
        return copy(at.at[p, j], a1.at[p, j], a1_s.at[p, j], a1_r.at[p, j], 0, own)

    def a_start(p):
        shard_go(at.at[p], a_s.at[p], a_r.at[p], 0)
        go(upper, lambda: across(p, z))

    def a_step(k, p):
        shard_wait(at.at[p], a_s.at[p], a_r.at[p], k)
        if k < lines - 1:
            shard_go(at.at[p], a_s.at[p], a_r.at[p], k)
        go((z >= k) & upper, lambda: across(p, z - k))
        go((z + k < lines) & upper, lambda: across(p, z + k))

    def b_step(k):
        shard_wait(bt, b_s, b_r, k)
        if k < lines - 1:
            shard_go(bt, b_s, b_r, k)

    def g_copy(k):
        return copy(
            sg.at[(h + k) % plane], rg.at[:, h], g_s.at[k - 1], g_r.at[k - 1], seg, host(k)
        )

    def x_copy(q, k):
        return copy(
            sx.at[q, (h + k) % plane], rx.at[q, :, h], x_s.at[q, k - 1], x_r.at[q, k - 1], seg, host(k)
        )

    shard_go(bt, b_s, b_r, 0)
    for k in range(1, plane):
        go(None, functools.partial(g_copy, k))
    rg[:, h] = sg[h]
    for q in range(chunks):
        sx[q] = (
            dot_nn(placing, x[:, q * part : (q + 1) * part])
            .astype(bf16)
            .reshape(plane, lines, cap, part)
        )
        for k in range(1, plane):
            go(None, functools.partial(x_copy, q, k))
        rx[q, :, h] = sx[q, h]
        if q == 0:
            b_step(1)
            a_start(0)
            a_start(1)
    b_step(2)
    b_step(3)

    cf[...] = jnp.zeros_like(cf)
    for k in range(1, plane):
        g_copy(k).wait_recv()
    for j in range(lines):
        grads = rg[j].reshape(rows, out_width)
        cf[j, :, :rank_dim] = (adapter_scale * dot_nt(grads, bt[j])).astype(bf16)
        cft[j, :, :rows] = (adapter_scale * dot_nt(bt[j], grads)).astype(bf16)

    def coef_copy():
        return copy(cf, c1, c_s, c_r, 0, own)

    go(upper, coef_copy)

    def sums(value, cols, send_l, send_r, recv_l, recv_r, s_sem, r_sem):
        def left(t):
            return copy(send_l.at[t], recv_l.at[t], s_sem.at[0, t], r_sem.at[0, t], seg, own - plane)

        def right(t):
            return copy(send_r.at[t], recv_r.at[t], s_sem.at[1, t], r_sem.at[1, t], seg, own + plane)

        def hop(stage):
            for t in range(lines - 1 - stage):
                for goal, buf, got, make, cond in (
                    (t, send_l, recv_l, left, z == lines - 1 - stage),
                    (lines - 1 - t, send_r, recv_r, right, z == stage),
                ):
                    @pl.when(cond)
                    def _():
                        mine = value(goal)
                        if stage > 0:
                            make(goal).wait_recv()
                            mine += got[goal].astype(f32)
                        buf[goal] = mine.astype(bf16)

                    go(cond, functools.partial(make, goal))

        def finish(out):
            out[:, cols] = value(z)

            @pl.when(has_right)
            def _():
                left(z).wait_recv()
                out[:, cols] += recv_l[z].astype(f32)

            @pl.when(has_left)
            def _():
                right(z).wait_recv()
                out[:, cols] += recv_r[z].astype(f32)

        return hop, finish

    downs = [
        sums(
            lambda j, q=q: dot_nn(cft[j, :, :rows], rx[q, j].reshape(rows, part)),
            pl.ds(q * part, part),
            sl.at[q], sr.at[q], ql.at[q], qr.at[q], d_s.at[q], d_r.at[q],
        )
        for q in range(chunks)
    ]

    def down_stage(m):
        if m < chunks:
            for k in range(1, plane):
                x_copy(m, k).wait_recv()
        for stage in range(lines - 1):
            if 0 <= m - stage < chunks:
                downs[m - stage][0](stage)

    order = (z, z + 1 - 2 * (z % 2), 2 - z // 2, 3 - 3 * (z // 2))

    def t_copy(p, i, k):
        return copy(
            ts.at[p, order[i], (h + k) % plane], tr.at[p, h, order[i]],
            t_s.at[p, i, k - 1], t_r.at[p, i, k - 1], seg, host(k),
        )

    def term(i, p):
        j = order[i]
        mine = dot_nn(cf[j, :, :rank_dim], at[p, j]).astype(bf16)

        @pl.when(upper)
        def _():
            ts[p, j] = mine.reshape(plane, cap, wide)

        @pl.when(lower)
        def _():
            across(p, j).wait_recv()
            above = dot_nn(c1[j, :, :rank_dim], a1[p, j]).astype(bf16)
            total = (mine.astype(f32) + above.astype(f32)).astype(bf16)
            ts[p, j] = total.reshape(plane, cap, wide)

        for k in range(1, plane):
            go(None, functools.partial(t_copy, p, i, k))
        tr[p, h, j] = ts[p, j, h]

    def project(i):
        j = order[i]
        proj = jnp.zeros((rank_dim, rows), f32)
        for q in range(chunks):
            p, first = q * part // wide, q * part % wide
            proj += dot_nt(at[p, j, :, first : first + part], rx[q, j].reshape(rows, part))
        gup[j] = dot_nn(proj.astype(bf16), rg[j].reshape(rows, out_width))

    up_hop, up_finish = sums(
        lambda j: gup[j], pl.ds(0, out_width), ul, ur, vl, vr, u_s, u_r
    )
    down_stage(0)
    a_step(1, 0)
    down_stage(1)
    a_step(1, 1)
    down_stage(2)
    a_step(2, 0)
    down_stage(3)
    a_step(2, 1)
    pl.when(lower)(lambda: coef_copy().wait_recv())
    term(0, 0)
    term(0, 1)
    down_stage(4)
    term(1, 0)
    term(1, 1)
    down_stage(5)
    project(0)
    project(1)
    a_step(3, 0)
    a_step(3, 1)
    project(2)
    project(3)
    up_hop(0)
    term(2, 0)
    term(2, 1)
    up_hop(1)
    term(3, 0)
    up_hop(2)
    term(3, 1)
    for _, finish in downs:
        finish(gd)
    up_finish(gu)
    for p in range(parts):
        for i in range(lines):
            for k in range(1, plane):
                t_copy(p, i, k).wait_recv()
        passed[:, p * wide : (p + 1) * wide] = dot_nn(
            placing_t, tr[p].reshape(plane * lines * cap, wide)
        ).astype(bf16)
    for cond, make in pending:
        if cond is None:
            make().wait_send()
        else:
            pl.when(cond)(functools.partial(lambda make: make().wait_send(), make))


def local_lines(
    layer_input_rows,
    output_gradient,
    tenant,
    adapter_owner_index,
    adapter_down_weight,
    adapter_up_weight,
):
    x, g = layer_input_rows[0], output_gradient[0]
    tok, width = x.shape
    out_width = g.shape[1]
    rank_dim = adapter_up_weight.shape[2]
    cap = 2 * tok // (lines * plane)
    rows = plane * cap
    part = width // chunks
    wide = width // parts
    lanes = 128
    vmem = pl.BlockSpec(memory_space=pltpu.VMEM)
    dma = pltpu.SemaphoreType.DMA
    passed, gd, gu = pl.pallas_call(
        lines_kernel,
        out_shape=(
            jax.ShapeDtypeStruct((tok, width), bf16),
            jax.ShapeDtypeStruct((rank_dim, width), f32),
            jax.ShapeDtypeStruct((rank_dim, out_width), f32),
        ),
        in_specs=[vmem] * 6,
        out_specs=(vmem,) * 3,
        scratch_shapes=[
            pltpu.VMEM((chunks, plane, lines, cap, part), bf16),
            pltpu.VMEM((plane, lines, cap, out_width), bf16),
            pltpu.VMEM((chunks, lines, plane, cap, part), bf16),
            pltpu.VMEM((lines, plane, cap, out_width), bf16),
            pltpu.VMEM((parts, lines, rank_dim, wide), bf16),
            pltpu.VMEM((lines, rank_dim, out_width), bf16),
            pltpu.VMEM((parts, lines, rank_dim, wide), bf16),
            pltpu.VMEM((lines, rows, lanes), bf16),
            pltpu.VMEM((lines, rank_dim, lanes), bf16),
            pltpu.VMEM((lines, rows, lanes), bf16),
            pltpu.VMEM((parts, lines, plane, cap, wide), bf16),
            pltpu.VMEM((parts, plane, lines, cap, wide), bf16),
        ]
        + [pltpu.VMEM((chunks, lines, rank_dim, part), bf16)] * 4
        + [pltpu.VMEM((lines, rank_dim, out_width), bf16)] * 4
        + [
            pltpu.VMEM((lines, rank_dim, out_width), f32),
            dma((chunks, plane - 1)), dma((chunks, plane - 1)),
            dma((plane - 1,)), dma((plane - 1,)),
            dma((parts, 2, lines)), dma((parts, lines)),
            dma((2, lines)), dma((lines,)),
            dma((parts, lines)), dma((parts, lines)),
            dma, dma,
            dma((parts, lines, plane - 1)), dma((parts, lines, plane - 1)),
            dma((chunks, 2, lines)), dma((chunks, 2, lines)),
            dma((2, lines)), dma((2, lines)),
        ],
        compiler_params=pltpu.CompilerParams(
            collective_id=0, has_side_effects=True, vmem_limit_bytes=56 * 1024 * 1024
        ),
        name="adapter_lines",
    )(
        x,
        g,
        tenant.reshape(1, tok),
        adapter_owner_index.reshape(1, -1),
        adapter_down_weight[0, 0].T,
        adapter_up_weight[0, 0],
    )
    return (passed[None], gd.T[None, None], gu[None, None])


def solution(mesh):
    planned = mesh.shape["segment"] == 2 and mesh.shape["owner"] == lines * plane
    return jax.shard_map(
        local_lines if planned else local,
        mesh=mesh,
        in_specs=(
            P("segment", "owner", None),
            P("segment", "owner", None),
            P("owner", None),
            P(),
            P("segment", "owner", None, None),
            P("segment", "owner", None, None),
        ),
        out_specs=(
            P("segment", "owner", None),
            P("segment", "owner", None, None),
            P("segment", "owner", None, None),
        ),
        check_vma=False,
    )
```

```python
import functools

import jax
import jax.numpy as jnp
from jax import lax
from jax.experimental import pallas as pl
from jax.experimental.pallas import tpu as pltpu
from jax.sharding import PartitionSpec as P

adapter_scale = 2.0


def prefix(x, axis, join, neutral):
    count = lax.axis_size(axis)
    place = lax.axis_index(axis)
    ahead = count - 1 - place
    gathered = lax.all_gather(x.astype(jnp.bfloat16), axis)
    state = jnp.zeros_like(x) + jnp.asarray(neutral, x.dtype)

    def one(step, state):
        source = count - 1 - step
        return join(state, lax.dynamic_index_in_dim(gathered, source, 0, False).astype(x.dtype))

    return lax.fori_loop(0, ahead, one, state)


def local(
    layer_input_rows,
    output_gradient,
    tenant,
    adapter_owner_index,
    adapter_down_weight,
    adapter_up_weight,
):
    inputs = layer_input_rows[0]
    gradient_list = output_gradient[0]
    tok_rows = inputs.shape[0]
    width = inputs.shape[1]
    out_width = gradient_list.shape[1]
    owners = lax.axis_size("owner")
    capacity = 2 * tok_rows // owners
    highest_precision = lax.Precision.HIGHEST
    ids = tenant[:, 0]
    adapter_count = adapter_owner_index.shape[0]
    matched = ids[:, None] == jnp.arange(adapter_count, dtype=jnp.int32)[None, :]
    dest = jnp.sum(jnp.where(matched, adapter_owner_index[None, :], 0), axis=1)
    onehot = (dest[:, None] == jnp.arange(owners, dtype=jnp.int32)[None, :]).astype(jnp.int32)
    rank = jnp.sum((jnp.cumsum(onehot, axis=0) - 1) * onehot, axis=1)
    target = dest * capacity + rank
    placing = (jnp.arange(owners * capacity, dtype=jnp.int32)[:, None] == target[None, :]).astype(
        jnp.bfloat16
    )
    send_inputs = jnp.dot(placing, inputs, preferred_element_type=jnp.float32).astype(jnp.bfloat16)
    send_grads = jnp.dot(placing, gradient_list, preferred_element_type=jnp.float32).astype(
        jnp.bfloat16
    )
    send_inputs = send_inputs.reshape(owners, capacity, width)
    send_grads = send_grads.reshape(owners, capacity, out_width)
    down_factor = adapter_down_weight[0, 0]
    up_factor = adapter_up_weight[0, 0]
    recv_inputs, recv_grads = (
        lax.all_to_all(send_inputs, "owner", split_axis=0, concat_axis=0, tiled=True),
        lax.all_to_all(send_grads, "owner", split_axis=0, concat_axis=0, tiled=True),
    )
    rows_in = recv_inputs.reshape(owners * capacity, width)
    rows_grad = recv_grads.reshape(owners * capacity, out_width)
    scale_weight = adapter_scale * jnp.einsum(
        "rm,km->rk", rows_grad, up_factor, preferred_element_type=jnp.float32
    )
    partial_terms = jnp.einsum(
        "rk,dk->rd",
        scale_weight,
        down_factor,
        precision=highest_precision,
        preferred_element_type=jnp.float32,
    )
    partial_terms = partial_terms.astype(jnp.bfloat16).reshape(owners, capacity, width)
    returned = lax.all_to_all(partial_terms, "owner", split_axis=0, concat_axis=0, tiled=True)
    projected_rows = jnp.dot(rows_in, down_factor, preferred_element_type=jnp.float32)
    grad_down = jnp.einsum(
        "rd,rk->dk",
        rows_in,
        scale_weight,
        precision=highest_precision,
        preferred_element_type=jnp.float32,
    )
    grad_up = jnp.einsum(
        "rk,rm->km",
        projected_rows,
        rows_grad,
        precision=highest_precision,
        preferred_element_type=jnp.float32,
    )
    own_term = jnp.einsum(
        "sr,sd->rd",
        placing,
        returned.reshape(owners * capacity, width),
        preferred_element_type=jnp.float32,
    )

    def combine(earlier, later):
        return earlier + later

    above = prefix(own_term, "segment", combine, jnp.zeros_like(own_term))
    passed = (above + own_term).astype(jnp.bfloat16)
    return (passed[None], grad_down[None, None], grad_up[None, None])


lines = 4
plane = 4
chunks = 4
parts = 2
bf16 = jnp.bfloat16
f32 = jnp.float32


def dot_nt(a, b):
    return lax.dot_general(a, b, (((1,), (1,)), ((), ())), preferred_element_type=f32)


def dot_nn(a, b):
    return jnp.dot(a, b, preferred_element_type=f32)


def lines_kernel(
    x, g, ids, owner_of, a, b,
    passed, gd, gu,
    sx, sg, rx, rg, at, bt, cf, cft, c1, ts, tr, sl, sr, ql, qr, ul, ur, vl, vr, gup,
    x_s, x_r, g_s, g_r, a_s, a_r, b_s, b_r, a1_s, a1_r, c_s, c_r, t_s, t_r, d_s, d_r, u_s, u_r,
):
    tok, width = x.shape
    out_width = g.shape[1]
    part = width // chunks
    wide = width // parts
    cap = sx.shape[3]
    rank_dim = b.shape[0]
    rows = plane * cap
    seg = lax.axis_index("segment")
    own = lax.axis_index("owner")
    z = own // plane
    h = own % plane
    upper = seg == 1
    lower = seg == 0
    pending = []

    def signal(segment, owner):
        pl.semaphore_signal(
            barrier, inc=1, device_id=(segment, owner), device_id_type=pl.DeviceIdType.MESH
        )

    def copy(source, sink, send, recv, segment, owner):
        return pltpu.make_async_remote_copy(
            src_ref=source, dst_ref=sink, send_sem=send, recv_sem=recv,
            device_id=(segment, owner), device_id_type=pl.DeviceIdType.MESH,
        )

    def go(cond, make):
        if cond is None:
            make().start()
        else:
            pl.when(cond)(lambda: make().start())
        pending.append((cond, make))

    def host(k):
        return z * plane + (h + k) % plane

    has_left = z > 0
    has_right = z < lines - 1

    barrier = pltpu.get_barrier_semaphore()
    for k in range(1, plane):
        signal(seg, host(k))
    signal(1 - seg, own)
    pl.when(has_left)(lambda: signal(seg, own - plane))
    pl.when(has_right)(lambda: signal(seg, own + plane))

    n_owner = lines * plane
    n_adapter = owner_of.shape[1]
    square = (n_adapter, n_adapter)
    diagonal = lax.broadcasted_iota(jnp.int32, square, 0) == lax.broadcasted_iota(jnp.int32, square, 1)
    owner_column = jnp.sum(jnp.where(diagonal, owner_of[...], 0), axis=1, keepdims=True)
    matched = lax.broadcasted_iota(jnp.int32, (n_adapter, tok), 0) == ids[...]
    dest = jnp.sum(jnp.where(matched, owner_column, 0), axis=0, keepdims=True)
    onehot = (lax.broadcasted_iota(jnp.int32, (n_owner, tok), 0) == dest).astype(f32)
    earlier = (
        lax.broadcasted_iota(jnp.int32, (tok, tok), 0)
        < lax.broadcasted_iota(jnp.int32, (tok, tok), 1)
    ).astype(f32)
    count = dot_nn(onehot.astype(bf16), earlier.astype(bf16))
    rank = jnp.sum(count * onehot, axis=0, keepdims=True).astype(jnp.int32)
    target = (dest % plane) * (lines * cap) + (dest // plane) * cap + rank
    placing32 = (
        lax.broadcasted_iota(jnp.int32, (plane * lines * cap, tok), 0) == target
    ).astype(f32)
    placing = placing32.astype(bf16)
    placing_t = placing32.T.astype(bf16)

    bt[z] = b[...]
    for p in range(parts):
        at[p, z, :rank_dim] = a[:, p * wide : (p + 1) * wide]
    sg[...] = dot_nn(placing, g[...]).astype(bf16).reshape(plane, lines, cap, out_width)
    pl.semaphore_wait(
        barrier, plane + jnp.where(has_left, 1, 0) + jnp.where(has_right, 1, 0)
    )

    def shard_right(view, send, recv, k):
        ref = view(z - k)
        return copy(ref, ref, send.at[0, k], recv.at[z - k], seg, own + plane)

    def shard_left(view, send, recv, k):
        ref = view(z + k)
        return copy(ref, ref, send.at[1, k], recv.at[z + k], seg, own - plane)

    def shard_go(view, send, recv, k):
        go((z >= k) & has_right, lambda: shard_right(view, send, recv, k))
        go((z + k < lines) & has_left, lambda: shard_left(view, send, recv, k))

    def shard_wait(view, send, recv, k):
        pl.when(z >= k)(lambda: shard_right(view, send, recv, k).wait_recv())
        pl.when(z + k < lines)(lambda: shard_left(view, send, recv, k).wait_recv())

    def b_view(j):
        return bt.at[j]

    def a_view(p):
        return lambda j: at.at[p, j, pl.ds(0, rank_dim)]

    def across(p, j):
        return copy(
            at.at[p, j, pl.ds(0, rank_dim)], at.at[p, j, pl.ds(rank_dim, rank_dim)],
            a1_s.at[p, j], a1_r.at[p, j], 0, own,
        )

    def a_start(p):
        shard_go(a_view(p), a_s.at[p], a_r.at[p], 0)
        go(upper, lambda: across(p, z))

    def a_step(k, p):
        shard_wait(a_view(p), a_s.at[p], a_r.at[p], k)
        if k < lines - 1:
            shard_go(a_view(p), a_s.at[p], a_r.at[p], k)
        go((z >= k) & upper, lambda: across(p, z - k))
        go((z + k < lines) & upper, lambda: across(p, z + k))

    def b_step(k):
        shard_wait(b_view, b_s, b_r, k)
        if k < lines - 1:
            shard_go(b_view, b_s, b_r, k)

    def g_copy(k):
        return copy(
            sg.at[(h + k) % plane], rg.at[:, h], g_s.at[k - 1], g_r.at[k - 1], seg, host(k)
        )

    def x_copy(q, k):
        return copy(
            sx.at[q, (h + k) % plane], rx.at[q, :, h], x_s.at[q, k - 1], x_r.at[q, k - 1], seg, host(k)
        )

    shard_go(b_view, b_s, b_r, 0)
    for k in range(1, plane):
        go(None, functools.partial(g_copy, k))
    rg[:, h] = sg[h]
    for q in range(chunks):
        sx[q] = (
            dot_nn(placing, x[:, q * part : (q + 1) * part])
            .astype(bf16)
            .reshape(plane, lines, cap, part)
        )
        for k in range(1, plane):
            go(None, functools.partial(x_copy, q, k))
        rx[q, :, h] = sx[q, h]
        if q == 0:
            b_step(1)
        if q == 1:
            b_step(2)
            a_start(0)
            a_start(1)
    b_step(3)

    for k in range(1, plane):
        g_copy(k).wait_recv()
    for j in range(lines):
        grads = rg[j].reshape(rows, out_width)
        cft[j, :, :rows] = (adapter_scale * dot_nt(bt[j], grads)).astype(bf16)

    def coef_copy():
        return copy(cf, c1, c_s, c_r, 0, own)

    def sums(value, cols, send_l, send_r, recv_l, recv_r, s_sem, r_sem):
        def left(t):
            return copy(send_l.at[t], recv_l.at[t], s_sem.at[0, t], r_sem.at[0, t], seg, own - plane)

        def right(t):
            return copy(send_r.at[t], recv_r.at[t], s_sem.at[1, t], r_sem.at[1, t], seg, own + plane)

        def hop(stage):
            for t in range(lines - 1 - stage):
                for goal, buf, got, make, cond in (
                    (t, send_l, recv_l, left, z == lines - 1 - stage),
                    (lines - 1 - t, send_r, recv_r, right, z == stage),
                ):
                    @pl.when(cond)
                    def _():
                        mine = value(goal)
                        if stage > 0:
                            make(goal).wait_recv()
                            mine += got[goal].astype(f32)
                        buf[goal] = mine.astype(bf16)

                    go(cond, functools.partial(make, goal))

        def finish(out):
            out[:, cols] = value(z)

            @pl.when(has_right)
            def _():
                left(z).wait_recv()
                out[:, cols] += recv_l[z].astype(f32)

            @pl.when(has_left)
            def _():
                right(z).wait_recv()
                out[:, cols] += recv_r[z].astype(f32)

        return hop, finish

    downs = [
        sums(
            lambda j, q=q: dot_nn(cft[j, :, :rows], rx[q, j].reshape(rows, part)),
            pl.ds(q * part, part),
            sl.at[q], sr.at[q], ql.at[q], qr.at[q], d_s.at[q], d_r.at[q],
        )
        for q in range(chunks)
    ]

    def down_stage(m):
        if m < chunks:
            for k in range(1, plane):
                x_copy(m, k).wait_recv()
        for stage in range(lines - 1):
            if 0 <= m - stage < chunks:
                downs[m - stage][0](stage)

    order = (z, z + 1 - 2 * (z % 2), 2 - z // 2, 3 - 3 * (z // 2))

    def t_copy(p, i, k):
        return copy(
            ts.at[p, order[i], (h + k) % plane], tr.at[p, h, order[i]],
            t_s.at[p, i, k - 1], t_r.at[p, i, k - 1], seg, host(k),
        )

    def term(i, p):
        j = order[i]

        @pl.when(upper)
        def _():
            total = dot_nn(cf[j, :, :rank_dim], at[p, j, :rank_dim])
            ts[p, j] = total.astype(bf16).reshape(plane, cap, wide)

        @pl.when(lower)
        def _():
            across(p, j).wait_recv()
            total = dot_nn(cf[j, :, : 2 * rank_dim], at[p, j])
            ts[p, j] = total.astype(bf16).reshape(plane, cap, wide)

        for k in range(1, plane):
            go(None, functools.partial(t_copy, p, i, k))
        tr[p, h, j] = ts[p, j, h]

    def project(i):
        j = order[i]
        proj = jnp.zeros((rank_dim, rows), f32)
        for q in range(chunks):
            p, first = q * part // wide, q * part % wide
            proj += dot_nt(at[p, j, :rank_dim, first : first + part], rx[q, j].reshape(rows, part))
        gup[j] = dot_nn(proj.astype(bf16), rg[j].reshape(rows, out_width))

    up_hop, up_finish = sums(
        lambda j: gup[j], pl.ds(0, out_width), ul, ur, vl, vr, u_s, u_r
    )
    down_stage(0)
    cf[...] = jnp.zeros_like(cf)
    for j in range(lines):
        grads = rg[j].reshape(rows, out_width)
        cf[j, :, :rank_dim] = (adapter_scale * dot_nt(grads, bt[j])).astype(bf16)
    go(upper, coef_copy)
    a_step(1, 0)
    down_stage(1)
    a_step(1, 1)
    down_stage(2)
    a_step(2, 0)
    down_stage(3)
    a_step(2, 1)

    @pl.when(lower)
    def _():
        coef_copy().wait_recv()
        cf[:, :, rank_dim : 2 * rank_dim] = c1[:, :, :rank_dim]

    term(0, 0)
    term(0, 1)
    down_stage(4)
    term(1, 0)
    term(1, 1)
    down_stage(5)
    project(0)
    project(1)
    a_step(3, 0)
    a_step(3, 1)
    project(2)
    project(3)
    up_hop(0)
    term(2, 0)
    term(2, 1)
    up_hop(1)
    term(3, 0)
    up_hop(2)
    term(3, 1)
    for _, finish in downs:
        finish(gd)
    up_finish(gu)
    for p in range(parts):
        for i in range(lines):
            for k in range(1, plane):
                t_copy(p, i, k).wait_recv()
        passed[:, p * wide : (p + 1) * wide] = dot_nn(
            placing_t, tr[p].reshape(plane * lines * cap, wide)
        ).astype(bf16)
    for cond, make in pending:
        if cond is None:
            make().wait_send()
        else:
            pl.when(cond)(functools.partial(lambda make: make().wait_send(), make))


def local_lines(
    layer_input_rows,
    output_gradient,
    tenant,
    adapter_owner_index,
    adapter_down_weight,
    adapter_up_weight,
):
    x, g = layer_input_rows[0], output_gradient[0]
    tok, width = x.shape
    out_width = g.shape[1]
    rank_dim = adapter_up_weight.shape[2]
    cap = 2 * tok // (lines * plane)
    rows = plane * cap
    part = width // chunks
    wide = width // parts
    lanes = 128
    vmem = pl.BlockSpec(memory_space=pltpu.VMEM)
    dma = pltpu.SemaphoreType.DMA
    passed, gd, gu = pl.pallas_call(
        lines_kernel,
        out_shape=(
            jax.ShapeDtypeStruct((tok, width), bf16),
            jax.ShapeDtypeStruct((rank_dim, width), f32),
            jax.ShapeDtypeStruct((rank_dim, out_width), f32),
        ),
        in_specs=[vmem] * 6,
        out_specs=(vmem,) * 3,
        scratch_shapes=[
            pltpu.VMEM((chunks, plane, lines, cap, part), bf16),
            pltpu.VMEM((plane, lines, cap, out_width), bf16),
            pltpu.VMEM((chunks, lines, plane, cap, part), bf16),
            pltpu.VMEM((lines, plane, cap, out_width), bf16),
            pltpu.VMEM((parts, lines, 2 * rank_dim, wide), bf16),
            pltpu.VMEM((lines, rank_dim, out_width), bf16),
            pltpu.VMEM((lines, rows, lanes), bf16),
            pltpu.VMEM((lines, rank_dim, lanes), bf16),
            pltpu.VMEM((lines, rows, lanes), bf16),
            pltpu.VMEM((parts, lines, plane, cap, wide), bf16),
            pltpu.VMEM((parts, plane, lines, cap, wide), bf16),
        ]
        + [pltpu.VMEM((chunks, lines, rank_dim, part), bf16)] * 4
        + [pltpu.VMEM((lines, rank_dim, out_width), bf16)] * 4
        + [
            pltpu.VMEM((lines, rank_dim, out_width), f32),
            dma((chunks, plane - 1)), dma((chunks, plane - 1)),
            dma((plane - 1,)), dma((plane - 1,)),
            dma((parts, 2, lines)), dma((parts, lines)),
            dma((2, lines)), dma((lines,)),
            dma((parts, lines)), dma((parts, lines)),
            dma, dma,
            dma((parts, lines, plane - 1)), dma((parts, lines, plane - 1)),
            dma((chunks, 2, lines)), dma((chunks, 2, lines)),
            dma((2, lines)), dma((2, lines)),
        ],
        compiler_params=pltpu.CompilerParams(
            collective_id=0, has_side_effects=True, vmem_limit_bytes=56 * 1024 * 1024
        ),
        name="adapter_lines",
    )(
        x,
        g,
        tenant.reshape(1, tok),
        adapter_owner_index.reshape(1, -1),
        adapter_down_weight[0, 0].T,
        adapter_up_weight[0, 0],
    )
    return (passed[None], gd.T[None, None], gu[None, None])


def solution(mesh):
    planned = mesh.shape["segment"] == 2 and mesh.shape["owner"] == lines * plane
    return jax.shard_map(
        local_lines if planned else local,
        mesh=mesh,
        in_specs=(
            P("segment", "owner", None),
            P("segment", "owner", None),
            P("owner", None),
            P(),
            P("segment", "owner", None, None),
            P("segment", "owner", None, None),
        ),
        out_specs=(
            P("segment", "owner", None),
            P("segment", "owner", None, None),
            P("segment", "owner", None, None),
        ),
        check_vma=False,
    )
```

```python
import functools

import jax
import jax.numpy as jnp
from jax import lax
from jax.experimental import pallas as pl
from jax.experimental.pallas import tpu as pltpu
from jax.sharding import PartitionSpec as P

adapter_scale = 2.0


def prefix(x, axis, join, neutral):
    count = lax.axis_size(axis)
    place = lax.axis_index(axis)
    ahead = count - 1 - place
    gathered = lax.all_gather(x.astype(jnp.bfloat16), axis)
    state = jnp.zeros_like(x) + jnp.asarray(neutral, x.dtype)

    def one(step, state):
        source = count - 1 - step
        return join(state, lax.dynamic_index_in_dim(gathered, source, 0, False).astype(x.dtype))

    return lax.fori_loop(0, ahead, one, state)


def local(
    layer_input_rows,
    output_gradient,
    tenant,
    adapter_owner_index,
    adapter_down_weight,
    adapter_up_weight,
):
    inputs = layer_input_rows[0]
    gradient_list = output_gradient[0]
    tok_rows = inputs.shape[0]
    width = inputs.shape[1]
    out_width = gradient_list.shape[1]
    owners = lax.axis_size("owner")
    capacity = 2 * tok_rows // owners
    highest_precision = lax.Precision.HIGHEST
    ids = tenant[:, 0]
    adapter_count = adapter_owner_index.shape[0]
    matched = ids[:, None] == jnp.arange(adapter_count, dtype=jnp.int32)[None, :]
    dest = jnp.sum(jnp.where(matched, adapter_owner_index[None, :], 0), axis=1)
    onehot = (dest[:, None] == jnp.arange(owners, dtype=jnp.int32)[None, :]).astype(jnp.int32)
    rank = jnp.sum((jnp.cumsum(onehot, axis=0) - 1) * onehot, axis=1)
    target = dest * capacity + rank
    placing = (jnp.arange(owners * capacity, dtype=jnp.int32)[:, None] == target[None, :]).astype(
        jnp.bfloat16
    )
    send_inputs = jnp.dot(placing, inputs, preferred_element_type=jnp.float32).astype(jnp.bfloat16)
    send_grads = jnp.dot(placing, gradient_list, preferred_element_type=jnp.float32).astype(
        jnp.bfloat16
    )
    send_inputs = send_inputs.reshape(owners, capacity, width)
    send_grads = send_grads.reshape(owners, capacity, out_width)
    down_factor = adapter_down_weight[0, 0]
    up_factor = adapter_up_weight[0, 0]
    recv_inputs, recv_grads = (
        lax.all_to_all(send_inputs, "owner", split_axis=0, concat_axis=0, tiled=True),
        lax.all_to_all(send_grads, "owner", split_axis=0, concat_axis=0, tiled=True),
    )
    rows_in = recv_inputs.reshape(owners * capacity, width)
    rows_grad = recv_grads.reshape(owners * capacity, out_width)
    scale_weight = adapter_scale * jnp.einsum(
        "rm,km->rk", rows_grad, up_factor, preferred_element_type=jnp.float32
    )
    partial_terms = jnp.einsum(
        "rk,dk->rd",
        scale_weight,
        down_factor,
        precision=highest_precision,
        preferred_element_type=jnp.float32,
    )
    partial_terms = partial_terms.astype(jnp.bfloat16).reshape(owners, capacity, width)
    returned = lax.all_to_all(partial_terms, "owner", split_axis=0, concat_axis=0, tiled=True)
    projected_rows = jnp.dot(rows_in, down_factor, preferred_element_type=jnp.float32)
    grad_down = jnp.einsum(
        "rd,rk->dk",
        rows_in,
        scale_weight,
        precision=highest_precision,
        preferred_element_type=jnp.float32,
    )
    grad_up = jnp.einsum(
        "rk,rm->km",
        projected_rows,
        rows_grad,
        precision=highest_precision,
        preferred_element_type=jnp.float32,
    )
    own_term = jnp.einsum(
        "sr,sd->rd",
        placing,
        returned.reshape(owners * capacity, width),
        preferred_element_type=jnp.float32,
    )

    def combine(earlier, later):
        return earlier + later

    above = prefix(own_term, "segment", combine, jnp.zeros_like(own_term))
    passed = (above + own_term).astype(jnp.bfloat16)
    return (passed[None], grad_down[None, None], grad_up[None, None])


lines = 4
plane = 4
chunks = 4
parts = 2
bf16 = jnp.bfloat16
f32 = jnp.float32


def dot_nt(a, b):
    return lax.dot_general(a, b, (((1,), (1,)), ((), ())), preferred_element_type=f32)


def dot_nn(a, b):
    return jnp.dot(a, b, preferred_element_type=f32)


def lines_kernel(
    x, g, ids, owner_of, a, b,
    passed, gd, gu,
    sx, sg, rx, rg, at, bt, cf, cft, c1, ts, tr, sl, sr, ql, qr, ul, ur, vl, vr, gup,
    x_s, x_r, g_s, g_r, a_s, a_r, b_s, b_r, a1_s, a1_r, c_s, c_r, t_s, t_r, d_s, d_r, u_s, u_r,
):
    tok, width = x.shape
    out_width = g.shape[1]
    part = width // chunks
    wide = width // parts
    cap = sx.shape[3]
    rank_dim = b.shape[0]
    rows = plane * cap
    seg = lax.axis_index("segment")
    own = lax.axis_index("owner")
    z = own // plane
    h = own % plane
    upper = seg == 1
    lower = seg == 0
    pending = []

    def signal(segment, owner):
        pl.semaphore_signal(
            barrier, inc=1, device_id=(segment, owner), device_id_type=pl.DeviceIdType.MESH
        )

    def copy(source, sink, send, recv, segment, owner):
        return pltpu.make_async_remote_copy(
            src_ref=source, dst_ref=sink, send_sem=send, recv_sem=recv,
            device_id=(segment, owner), device_id_type=pl.DeviceIdType.MESH,
        )

    def go(cond, make):
        if cond is None:
            make().start()
        else:
            pl.when(cond)(lambda: make().start())
        pending.append((cond, make))

    def host(k):
        return z * plane + (h + k) % plane

    has_left = z > 0
    has_right = z < lines - 1

    barrier = pltpu.get_barrier_semaphore()
    for k in range(1, plane):
        signal(seg, host(k))
    signal(1 - seg, own)
    pl.when(has_left)(lambda: signal(seg, own - plane))
    pl.when(has_right)(lambda: signal(seg, own + plane))

    n_owner = lines * plane
    n_adapter = owner_of.shape[1]
    square = (n_adapter, n_adapter)
    diagonal = lax.broadcasted_iota(jnp.int32, square, 0) == lax.broadcasted_iota(jnp.int32, square, 1)
    owner_column = jnp.sum(jnp.where(diagonal, owner_of[...], 0), axis=1, keepdims=True)
    matched = lax.broadcasted_iota(jnp.int32, (n_adapter, tok), 0) == ids[...]
    dest = jnp.sum(jnp.where(matched, owner_column, 0), axis=0, keepdims=True)
    onehot = (lax.broadcasted_iota(jnp.int32, (n_owner, tok), 0) == dest).astype(f32)
    earlier = (
        lax.broadcasted_iota(jnp.int32, (tok, tok), 0)
        < lax.broadcasted_iota(jnp.int32, (tok, tok), 1)
    ).astype(f32)
    count = dot_nn(onehot.astype(bf16), earlier.astype(bf16))
    rank = jnp.sum(count * onehot, axis=0, keepdims=True).astype(jnp.int32)
    target = (dest % plane) * (lines * cap) + (dest // plane) * cap + rank
    placing32 = (
        lax.broadcasted_iota(jnp.int32, (plane * lines * cap, tok), 0) == target
    ).astype(f32)
    placing = placing32.astype(bf16)
    placing_t = placing32.T.astype(bf16)

    bt[z] = b[...]
    for p in range(parts):
        at[p, z, :rank_dim] = a[:, p * wide : (p + 1) * wide]
    sg[...] = dot_nn(placing, g[...]).astype(bf16).reshape(plane, lines, cap, out_width)
    pl.semaphore_wait(
        barrier, plane + jnp.where(has_left, 1, 0) + jnp.where(has_right, 1, 0)
    )

    def shard_right(view, send, recv, k):
        ref = view(z - k)
        return copy(ref, ref, send.at[0, k], recv.at[z - k], seg, own + plane)

    def shard_left(view, send, recv, k):
        ref = view(z + k)
        return copy(ref, ref, send.at[1, k], recv.at[z + k], seg, own - plane)

    def shard_go(view, send, recv, k):
        go((z >= k) & has_right, lambda: shard_right(view, send, recv, k))
        go((z + k < lines) & has_left, lambda: shard_left(view, send, recv, k))

    def shard_wait(view, send, recv, k):
        pl.when(z >= k)(lambda: shard_right(view, send, recv, k).wait_recv())
        pl.when(z + k < lines)(lambda: shard_left(view, send, recv, k).wait_recv())

    def b_view(j):
        return bt.at[j]

    def a_view(p):
        return lambda j: at.at[p, j, pl.ds(0, rank_dim)]

    def across(p, j):
        return copy(
            at.at[p, j, pl.ds(0, rank_dim)], at.at[p, j, pl.ds(rank_dim, rank_dim)],
            a1_s.at[p, j], a1_r.at[p, j], 0, own,
        )

    def a_start(p):
        shard_go(a_view(p), a_s.at[p], a_r.at[p], 0)

    def a_step(k, p):
        shard_wait(a_view(p), a_s.at[p], a_r.at[p], k)
        if k < lines - 1:
            shard_go(a_view(p), a_s.at[p], a_r.at[p], k)
        go((z >= k) & upper, lambda: across(p, z - k))
        go((z + k < lines) & upper, lambda: across(p, z + k))

    def b_step(k):
        shard_wait(b_view, b_s, b_r, k)
        if k < lines - 1:
            shard_go(b_view, b_s, b_r, k)

    def g_copy(k):
        return copy(
            sg.at[(h + k) % plane], rg.at[:, h], g_s.at[k - 1], g_r.at[k - 1], seg, host(k)
        )

    def x_copy(q, k):
        return copy(
            sx.at[q, (h + k) % plane], rx.at[q, :, h], x_s.at[q, k - 1], x_r.at[q, k - 1], seg, host(k)
        )

    shard_go(b_view, b_s, b_r, 0)
    for p in range(parts):
        go(upper, functools.partial(across, p, z))
    for k in range(1, plane):
        go(None, functools.partial(g_copy, k))
    rg[:, h] = sg[h]
    for q in range(chunks):
        sx[q] = (
            dot_nn(placing, x[:, q * part : (q + 1) * part])
            .astype(bf16)
            .reshape(plane, lines, cap, part)
        )
        for k in range(1, plane):
            go(None, functools.partial(x_copy, q, k))
        rx[q, :, h] = sx[q, h]
        if q == 0:
            b_step(1)
        if q == 1:
            b_step(2)
            a_start(0)
            a_start(1)
    b_step(3)

    for k in range(1, plane):
        g_copy(k).wait_recv()
    for j in range(lines):
        grads = rg[j].reshape(rows, out_width)
        cft[j, :, :rows] = (adapter_scale * dot_nt(bt[j], grads)).astype(bf16)

    def coef_copy():
        return copy(cf, c1, c_s, c_r, 0, own)

    def sums(value, cols, send_l, send_r, recv_l, recv_r, s_sem, r_sem):
        def left(t):
            return copy(send_l.at[t], recv_l.at[t], s_sem.at[0, t], r_sem.at[0, t], seg, own - plane)

        def right(t):
            return copy(send_r.at[t], recv_r.at[t], s_sem.at[1, t], r_sem.at[1, t], seg, own + plane)

        def hop(stage):
            for t in range(lines - 1 - stage):
                for goal, buf, got, make, cond in (
                    (t, send_l, recv_l, left, z == lines - 1 - stage),
                    (lines - 1 - t, send_r, recv_r, right, z == stage),
                ):
                    @pl.when(cond)
                    def _():
                        mine = value(goal)
                        if stage > 0:
                            make(goal).wait_recv()
                            mine += got[goal].astype(f32)
                        buf[goal] = mine.astype(bf16)

                    go(cond, functools.partial(make, goal))

        def finish(out):
            out[:, cols] = value(z)

            @pl.when(has_right)
            def _():
                left(z).wait_recv()
                out[:, cols] += recv_l[z].astype(f32)

            @pl.when(has_left)
            def _():
                right(z).wait_recv()
                out[:, cols] += recv_r[z].astype(f32)

        return hop, finish

    downs = [
        sums(
            lambda j, q=q: dot_nn(cft[j, :, :rows], rx[q, j].reshape(rows, part)),
            pl.ds(q * part, part),
            sl.at[q], sr.at[q], ql.at[q], qr.at[q], d_s.at[q], d_r.at[q],
        )
        for q in range(chunks)
    ]

    def down_stage(m):
        for q in {chunks - 2: (chunks - 2, chunks - 1)}.get(m, (m,) if m < chunks - 2 else ()):
            for k in range(1, plane):
                x_copy(q, k).wait_recv()
        for stage in range(lines - 1):
            if 0 <= m - stage < chunks:
                downs[m - stage][0](stage)

    order = (z, z + 1 - 2 * (z % 2), 2 - z // 2, 3 - 3 * (z // 2))

    def t_copy(p, i, k):
        return copy(
            ts.at[p, order[i], (h + k) % plane], tr.at[p, h, order[i]],
            t_s.at[p, i, k - 1], t_r.at[p, i, k - 1], seg, host(k),
        )

    def term(i, p):
        j = order[i]

        @pl.when(upper)
        def _():
            total = dot_nn(cf[j, :, :rank_dim], at[p, j, :rank_dim])
            ts[p, j] = total.astype(bf16).reshape(plane, cap, wide)

        @pl.when(lower)
        def _():
            across(p, j).wait_recv()
            total = dot_nn(cf[j, :, : 2 * rank_dim], at[p, j])
            ts[p, j] = total.astype(bf16).reshape(plane, cap, wide)

        for k in range(1, plane):
            go(None, functools.partial(t_copy, p, i, k))
        tr[p, h, j] = ts[p, j, h]

    def project(i):
        j = order[i]
        proj = jnp.zeros((rank_dim, rows), f32)
        for q in range(chunks):
            p, first = q * part // wide, q * part % wide
            proj += dot_nt(at[p, j, :rank_dim, first : first + part], rx[q, j].reshape(rows, part))
        gup[j] = dot_nn(proj.astype(bf16), rg[j].reshape(rows, out_width))

    up_hop, up_finish = sums(
        lambda j: gup[j], pl.ds(0, out_width), ul, ur, vl, vr, u_s, u_r
    )
    down_stage(0)
    cf[...] = jnp.zeros_like(cf)
    for j in range(lines):
        grads = rg[j].reshape(rows, out_width)
        cf[j, :, :rank_dim] = (adapter_scale * dot_nt(grads, bt[j])).astype(bf16)
    go(upper, coef_copy)
    a_step(1, 0)
    a_step(1, 1)
    down_stage(1)
    a_step(2, 0)
    a_step(2, 1)

    @pl.when(lower)
    def _():
        coef_copy().wait_recv()
        cf[:, :, rank_dim : 2 * rank_dim] = c1[:, :, :rank_dim]

    term(0, 0)
    term(0, 1)
    down_stage(2)
    project(0)
    project(1)
    a_step(3, 0)
    a_step(3, 1)
    term(1, 0)
    term(1, 1)
    down_stage(3)
    project(2)
    project(3)
    up_hop(0)
    term(2, 0)
    term(2, 1)
    down_stage(4)
    term(3, 0)
    up_hop(1)
    down_stage(5)
    term(3, 1)
    up_hop(2)
    for _, finish in downs:
        finish(gd)
    up_finish(gu)
    for p in range(parts):
        for i in range(lines):
            for k in range(1, plane):
                t_copy(p, i, k).wait_recv()
        passed[:, p * wide : (p + 1) * wide] = dot_nn(
            placing_t, tr[p].reshape(plane * lines * cap, wide)
        ).astype(bf16)
    for cond, make in pending:
        if cond is None:
            make().wait_send()
        else:
            pl.when(cond)(functools.partial(lambda make: make().wait_send(), make))


def local_lines(
    layer_input_rows,
    output_gradient,
    tenant,
    adapter_owner_index,
    adapter_down_weight,
    adapter_up_weight,
):
    x, g = layer_input_rows[0], output_gradient[0]
    tok, width = x.shape
    out_width = g.shape[1]
    rank_dim = adapter_up_weight.shape[2]
    cap = 2 * tok // (lines * plane)
    rows = plane * cap
    part = width // chunks
    wide = width // parts
    lanes = 128
    vmem = pl.BlockSpec(memory_space=pltpu.VMEM)
    dma = pltpu.SemaphoreType.DMA
    passed, gd, gu = pl.pallas_call(
        lines_kernel,
        out_shape=(
            jax.ShapeDtypeStruct((tok, width), bf16),
            jax.ShapeDtypeStruct((rank_dim, width), f32),
            jax.ShapeDtypeStruct((rank_dim, out_width), f32),
        ),
        in_specs=[vmem] * 6,
        out_specs=(vmem,) * 3,
        scratch_shapes=[
            pltpu.VMEM((chunks, plane, lines, cap, part), bf16),
            pltpu.VMEM((plane, lines, cap, out_width), bf16),
            pltpu.VMEM((chunks, lines, plane, cap, part), bf16),
            pltpu.VMEM((lines, plane, cap, out_width), bf16),
            pltpu.VMEM((parts, lines, 2 * rank_dim, wide), bf16),
            pltpu.VMEM((lines, rank_dim, out_width), bf16),
            pltpu.VMEM((lines, rows, lanes), bf16),
            pltpu.VMEM((lines, rank_dim, lanes), bf16),
            pltpu.VMEM((lines, rows, lanes), bf16),
            pltpu.VMEM((parts, lines, plane, cap, wide), bf16),
            pltpu.VMEM((parts, plane, lines, cap, wide), bf16),
        ]
        + [pltpu.VMEM((chunks, lines, rank_dim, part), bf16)] * 4
        + [pltpu.VMEM((lines, rank_dim, out_width), bf16)] * 4
        + [
            pltpu.VMEM((lines, rank_dim, out_width), f32),
            dma((chunks, plane - 1)), dma((chunks, plane - 1)),
            dma((plane - 1,)), dma((plane - 1,)),
            dma((parts, 2, lines)), dma((parts, lines)),
            dma((2, lines)), dma((lines,)),
            dma((parts, lines)), dma((parts, lines)),
            dma, dma,
            dma((parts, lines, plane - 1)), dma((parts, lines, plane - 1)),
            dma((chunks, 2, lines)), dma((chunks, 2, lines)),
            dma((2, lines)), dma((2, lines)),
        ],
        compiler_params=pltpu.CompilerParams(
            collective_id=0, has_side_effects=True, vmem_limit_bytes=56 * 1024 * 1024
        ),
        name="adapter_lines",
    )(
        x,
        g,
        tenant.reshape(1, tok),
        adapter_owner_index.reshape(1, -1),
        adapter_down_weight[0, 0].T,
        adapter_up_weight[0, 0],
    )
    return (passed[None], gd.T[None, None], gu[None, None])


def solution(mesh):
    planned = mesh.shape["segment"] == 2 and mesh.shape["owner"] == lines * plane
    return jax.shard_map(
        local_lines if planned else local,
        mesh=mesh,
        in_specs=(
            P("segment", "owner", None),
            P("segment", "owner", None),
            P("owner", None),
            P(),
            P("segment", "owner", None, None),
            P("segment", "owner", None, None),
        ),
        out_specs=(
            P("segment", "owner", None),
            P("segment", "owner", None, None),
            P("segment", "owner", None, None),
        ),
        check_vma=False,
    )
```

```python
import functools

import jax
import jax.numpy as jnp
from jax import lax
from jax.experimental import pallas as pl
from jax.experimental.pallas import tpu as pltpu
from jax.sharding import PartitionSpec as P

adapter_scale = 2.0


def prefix(x, axis, join, neutral):
    count = lax.axis_size(axis)
    place = lax.axis_index(axis)
    ahead = count - 1 - place
    gathered = lax.all_gather(x.astype(jnp.bfloat16), axis)
    state = jnp.zeros_like(x) + jnp.asarray(neutral, x.dtype)

    def one(step, state):
        source = count - 1 - step
        return join(state, lax.dynamic_index_in_dim(gathered, source, 0, False).astype(x.dtype))

    return lax.fori_loop(0, ahead, one, state)


def local(
    layer_input_rows,
    output_gradient,
    tenant,
    adapter_owner_index,
    adapter_down_weight,
    adapter_up_weight,
):
    inputs = layer_input_rows[0]
    gradient_list = output_gradient[0]
    tok_rows = inputs.shape[0]
    width = inputs.shape[1]
    out_width = gradient_list.shape[1]
    owners = lax.axis_size("owner")
    capacity = 2 * tok_rows // owners
    highest_precision = lax.Precision.HIGHEST
    ids = tenant[:, 0]
    adapter_count = adapter_owner_index.shape[0]
    matched = ids[:, None] == jnp.arange(adapter_count, dtype=jnp.int32)[None, :]
    dest = jnp.sum(jnp.where(matched, adapter_owner_index[None, :], 0), axis=1)
    onehot = (dest[:, None] == jnp.arange(owners, dtype=jnp.int32)[None, :]).astype(jnp.int32)
    rank = jnp.sum((jnp.cumsum(onehot, axis=0) - 1) * onehot, axis=1)
    target = dest * capacity + rank
    placing = (jnp.arange(owners * capacity, dtype=jnp.int32)[:, None] == target[None, :]).astype(
        jnp.bfloat16
    )
    send_inputs = jnp.dot(placing, inputs, preferred_element_type=jnp.float32).astype(jnp.bfloat16)
    send_grads = jnp.dot(placing, gradient_list, preferred_element_type=jnp.float32).astype(
        jnp.bfloat16
    )
    send_inputs = send_inputs.reshape(owners, capacity, width)
    send_grads = send_grads.reshape(owners, capacity, out_width)
    down_factor = adapter_down_weight[0, 0]
    up_factor = adapter_up_weight[0, 0]
    recv_inputs, recv_grads = (
        lax.all_to_all(send_inputs, "owner", split_axis=0, concat_axis=0, tiled=True),
        lax.all_to_all(send_grads, "owner", split_axis=0, concat_axis=0, tiled=True),
    )
    rows_in = recv_inputs.reshape(owners * capacity, width)
    rows_grad = recv_grads.reshape(owners * capacity, out_width)
    scale_weight = adapter_scale * jnp.einsum(
        "rm,km->rk", rows_grad, up_factor, preferred_element_type=jnp.float32
    )
    partial_terms = jnp.einsum(
        "rk,dk->rd",
        scale_weight,
        down_factor,
        precision=highest_precision,
        preferred_element_type=jnp.float32,
    )
    partial_terms = partial_terms.astype(jnp.bfloat16).reshape(owners, capacity, width)
    returned = lax.all_to_all(partial_terms, "owner", split_axis=0, concat_axis=0, tiled=True)
    projected_rows = jnp.dot(rows_in, down_factor, preferred_element_type=jnp.float32)
    grad_down = jnp.einsum(
        "rd,rk->dk",
        rows_in,
        scale_weight,
        precision=highest_precision,
        preferred_element_type=jnp.float32,
    )
    grad_up = jnp.einsum(
        "rk,rm->km",
        projected_rows,
        rows_grad,
        precision=highest_precision,
        preferred_element_type=jnp.float32,
    )
    own_term = jnp.einsum(
        "sr,sd->rd",
        placing,
        returned.reshape(owners * capacity, width),
        preferred_element_type=jnp.float32,
    )

    def combine(earlier, later):
        return earlier + later

    above = prefix(own_term, "segment", combine, jnp.zeros_like(own_term))
    passed = (above + own_term).astype(jnp.bfloat16)
    return (passed[None], grad_down[None, None], grad_up[None, None])


lines = 4
plane = 4
chunks = 4
parts = 2
bf16 = jnp.bfloat16
f32 = jnp.float32


def dot_nt(a, b):
    return lax.dot_general(a, b, (((1,), (1,)), ((), ())), preferred_element_type=f32)


def dot_nn(a, b):
    return jnp.dot(a, b, preferred_element_type=f32)


def lines_kernel(
    x, g, ids, owner_of, a, b,
    returned, back, gd, gu,
    sx, sg, rx, rg, at, bt, cf, cft, c1, ts, tr, sl, sr, ql, qr, ul, ur, vl, vr, gup,
    x_s, x_r, g_s, g_r, a_s, a_r, b_s, b_r, a1_s, a1_r, c_s, c_r, t_s, t_r, d_s, d_r, u_s, u_r, o_s,
):
    tok, width = x.shape
    out_width = g.shape[1]
    part = width // chunks
    wide = width // parts
    cap = sx.shape[3]
    rank_dim = b.shape[0]
    rows = plane * cap
    seg = lax.axis_index("segment")
    own = lax.axis_index("owner")
    z = own // plane
    h = own % plane
    upper = seg == 1
    lower = seg == 0
    pending = []

    def signal(segment, owner):
        pl.semaphore_signal(
            barrier, inc=1, device_id=(segment, owner), device_id_type=pl.DeviceIdType.MESH
        )

    def copy(source, sink, send, recv, segment, owner):
        return pltpu.make_async_remote_copy(
            src_ref=source, dst_ref=sink, send_sem=send, recv_sem=recv,
            device_id=(segment, owner), device_id_type=pl.DeviceIdType.MESH,
        )

    def go(cond, make):
        if cond is None:
            make().start()
        else:
            pl.when(cond)(lambda: make().start())
        pending.append((cond, make))

    def host(k):
        return z * plane + (h + k) % plane

    has_left = z > 0
    has_right = z < lines - 1

    barrier = pltpu.get_barrier_semaphore()
    for k in range(1, plane):
        signal(seg, host(k))
    signal(1 - seg, own)
    pl.when(has_left)(lambda: signal(seg, own - plane))
    pl.when(has_right)(lambda: signal(seg, own + plane))

    n_owner = lines * plane
    n_adapter = owner_of.shape[1]
    square = (n_adapter, n_adapter)
    diagonal = lax.broadcasted_iota(jnp.int32, square, 0) == lax.broadcasted_iota(jnp.int32, square, 1)
    owner_column = jnp.sum(jnp.where(diagonal, owner_of[...], 0), axis=1, keepdims=True)
    matched = lax.broadcasted_iota(jnp.int32, (n_adapter, tok), 0) == ids[...]
    dest = jnp.sum(jnp.where(matched, owner_column, 0), axis=0, keepdims=True)
    onehot = (lax.broadcasted_iota(jnp.int32, (n_owner, tok), 0) == dest).astype(f32)
    earlier = (
        lax.broadcasted_iota(jnp.int32, (tok, tok), 0)
        < lax.broadcasted_iota(jnp.int32, (tok, tok), 1)
    ).astype(f32)
    count = dot_nn(onehot.astype(bf16), earlier.astype(bf16))
    rank = jnp.sum(count * onehot, axis=0, keepdims=True).astype(jnp.int32)
    target = (dest % plane) * (lines * cap) + (dest // plane) * cap + rank
    placing32 = (
        lax.broadcasted_iota(jnp.int32, (plane * lines * cap, tok), 0) == target
    ).astype(f32)
    placing = placing32.astype(bf16)
    back[...] = placing32.T.astype(bf16)

    bt[z] = b[...]
    for p in range(parts):
        at[p, z, :rank_dim] = a[:, p * wide : (p + 1) * wide]
    sg[...] = dot_nn(placing, g[...]).astype(bf16).reshape(plane, lines, cap, out_width)
    pl.semaphore_wait(
        barrier, plane + jnp.where(has_left, 1, 0) + jnp.where(has_right, 1, 0)
    )

    def shard_right(view, send, recv, k):
        ref = view(z - k)
        return copy(ref, ref, send.at[0, k], recv.at[z - k], seg, own + plane)

    def shard_left(view, send, recv, k):
        ref = view(z + k)
        return copy(ref, ref, send.at[1, k], recv.at[z + k], seg, own - plane)

    def shard_go(view, send, recv, k):
        go((z >= k) & has_right, lambda: shard_right(view, send, recv, k))
        go((z + k < lines) & has_left, lambda: shard_left(view, send, recv, k))

    def shard_wait(view, send, recv, k):
        pl.when(z >= k)(lambda: shard_right(view, send, recv, k).wait_recv())
        pl.when(z + k < lines)(lambda: shard_left(view, send, recv, k).wait_recv())

    def b_view(j):
        return bt.at[j]

    def a_view(p):
        return lambda j: at.at[p, j, pl.ds(0, rank_dim)]

    def across(p, j):
        return copy(
            at.at[p, j, pl.ds(0, rank_dim)], at.at[p, j, pl.ds(rank_dim, rank_dim)],
            a1_s.at[p, j], a1_r.at[p, j], 0, own,
        )

    def a_start(p):
        shard_go(a_view(p), a_s.at[p], a_r.at[p], 0)

    def a_step(k, p):
        shard_wait(a_view(p), a_s.at[p], a_r.at[p], k)
        if k < lines - 1:
            shard_go(a_view(p), a_s.at[p], a_r.at[p], k)
        go((z >= k) & upper, lambda: across(p, z - k))
        go((z + k < lines) & upper, lambda: across(p, z + k))

    def b_step(k):
        shard_wait(b_view, b_s, b_r, k)
        if k < lines - 1:
            shard_go(b_view, b_s, b_r, k)

    def g_copy(k):
        return copy(
            sg.at[(h + k) % plane], rg.at[:, h], g_s.at[k - 1], g_r.at[k - 1], seg, host(k)
        )

    def x_copy(q, k):
        return copy(
            sx.at[q, (h + k) % plane], rx.at[q, :, h], x_s.at[q, k - 1], x_r.at[q, k - 1], seg, host(k)
        )

    shard_go(b_view, b_s, b_r, 0)
    for p in range(parts):
        go(upper, functools.partial(across, p, z))
    for k in range(1, plane):
        go(None, functools.partial(g_copy, k))
    rg[:, h] = sg[h]
    for q in range(chunks):
        sx[q] = (
            dot_nn(placing, x[:, q * part : (q + 1) * part])
            .astype(bf16)
            .reshape(plane, lines, cap, part)
        )
        for k in range(1, plane):
            go(None, functools.partial(x_copy, q, k))
        rx[q, :, h] = sx[q, h]
        if q == 0:
            b_step(1)
        if q == 1:
            b_step(2)
            a_start(0)
            a_start(1)
    b_step(3)

    for k in range(1, plane):
        g_copy(k).wait_recv()
    for j in range(lines):
        grads = rg[j].reshape(rows, out_width)
        cft[j, :, :rows] = (adapter_scale * dot_nt(bt[j], grads)).astype(bf16)

    def coef_copy():
        return copy(cf, c1, c_s, c_r, 0, own)

    def sums(value, cols, send_l, send_r, recv_l, recv_r, s_sem, r_sem):
        def left(t):
            return copy(send_l.at[t], recv_l.at[t], s_sem.at[0, t], r_sem.at[0, t], seg, own - plane)

        def right(t):
            return copy(send_r.at[t], recv_r.at[t], s_sem.at[1, t], r_sem.at[1, t], seg, own + plane)

        def hop(stage):
            for t in range(lines - 1 - stage):
                for goal, buf, got, make, cond in (
                    (t, send_l, recv_l, left, z == lines - 1 - stage),
                    (lines - 1 - t, send_r, recv_r, right, z == stage),
                ):
                    @pl.when(cond)
                    def _():
                        mine = value(goal)
                        if stage > 0:
                            make(goal).wait_recv()
                            mine += got[goal].astype(f32)
                        buf[goal] = mine.astype(bf16)

                    go(cond, functools.partial(make, goal))

        def finish(out):
            out[:, cols] = value(z)

            @pl.when(has_right)
            def _():
                left(z).wait_recv()
                out[:, cols] += recv_l[z].astype(f32)

            @pl.when(has_left)
            def _():
                right(z).wait_recv()
                out[:, cols] += recv_r[z].astype(f32)

        return hop, finish

    downs = [
        sums(
            lambda j, q=q: dot_nn(cft[j, :, :rows], rx[q, j].reshape(rows, part)),
            pl.ds(q * part, part),
            sl.at[q], sr.at[q], ql.at[q], qr.at[q], d_s.at[q], d_r.at[q],
        )
        for q in range(chunks)
    ]

    def down_hop(q, stage):
        if stage == 0:
            for k in range(1, plane):
                x_copy(q, k).wait_recv()
        downs[q][0](stage)

    order = (z, z + 1 - 2 * (z % 2), 2 - z // 2, 3 - 3 * (z // 2))

    def t_copy(p, i, k):
        return copy(
            ts.at[p, order[i], (h + k) % plane], tr.at[p, h, order[i]],
            t_s.at[p, i, k - 1], t_r.at[p, i, k - 1], seg, host(k),
        )

    def term(i, p):
        j = order[i]

        @pl.when(upper)
        def _():
            total = dot_nn(cf[j, :, :rank_dim], at[p, j, :rank_dim])
            ts[p, j] = total.astype(bf16).reshape(plane, cap, wide)

        @pl.when(lower)
        def _():
            across(p, j).wait_recv()
            total = dot_nn(cf[j, :, : 2 * rank_dim], at[p, j])
            ts[p, j] = total.astype(bf16).reshape(plane, cap, wide)

        for k in range(1, plane):
            go(None, functools.partial(t_copy, p, i, k))
        tr[p, h, j] = ts[p, j, h]

    def project(i):
        j = order[i]
        proj = jnp.zeros((rank_dim, rows), f32)
        for q in range(chunks):
            p, first = q * part // wide, q * part % wide
            proj += dot_nt(at[p, j, :rank_dim, first : first + part], rx[q, j].reshape(rows, part))
        gup[j] = dot_nn(proj.astype(bf16), rg[j].reshape(rows, out_width))

    up_hop, up_finish = sums(
        lambda j: gup[j], pl.ds(0, out_width), ul, ur, vl, vr, u_s, u_r
    )
    down_hop(0, 0)
    cf[...] = jnp.zeros_like(cf)
    for j in range(lines):
        grads = rg[j].reshape(rows, out_width)
        cf[j, :, :rank_dim] = (adapter_scale * dot_nt(grads, bt[j])).astype(bf16)
    go(upper, coef_copy)
    down_hop(1, 0)
    a_step(1, 0)
    a_step(1, 1)
    down_hop(2, 0)
    down_hop(0, 1)
    a_step(2, 0)
    down_hop(3, 0)
    a_step(2, 1)

    @pl.when(lower)
    def _():
        coef_copy().wait_recv()
        cf[:, :, rank_dim : 2 * rank_dim] = c1[:, :, :rank_dim]

    term(0, 0)
    term(0, 1)
    down_hop(1, 1)
    down_hop(0, 2)
    term(1, 0)
    term(1, 1)
    down_hop(2, 1)
    down_hop(1, 2)
    term(2, 0)
    term(2, 1)
    project(0)
    project(1)
    a_step(3, 0)
    a_step(3, 1)
    project(2)
    project(3)
    up_hop(0)
    down_hop(3, 1)
    down_hop(2, 2)
    term(3, 0)
    up_hop(1)
    down_hop(3, 2)
    term(3, 1)
    up_hop(2)
    for _, finish in downs:
        finish(gd)
    up_finish(gu)
    for p in range(parts):
        for i in range(lines):
            for k in range(1, plane):
                t_copy(p, i, k).wait_recv()
        pltpu.make_async_copy(tr.at[p], returned.at[p], o_s.at[p]).start()
    for p in range(parts):
        pltpu.make_async_copy(tr.at[p], returned.at[p], o_s.at[p]).wait()
    for cond, make in pending:
        if cond is None:
            make().wait_send()
        else:
            pl.when(cond)(functools.partial(lambda make: make().wait_send(), make))


def select_kernel(returned, back, gd_in, gu_in, passed, gd, gu):
    passed[...] = dot_nn(back[...], returned[0]).astype(bf16)
    gd[...] = gd_in[...]
    gu[...] = gu_in[...]


def local_lines(
    layer_input_rows,
    output_gradient,
    tenant,
    adapter_owner_index,
    adapter_down_weight,
    adapter_up_weight,
):
    x, g = layer_input_rows[0], output_gradient[0]
    tok, width = x.shape
    out_width = g.shape[1]
    rank_dim = adapter_up_weight.shape[2]
    cap = 2 * tok // (lines * plane)
    rows = plane * cap
    part = width // chunks
    wide = width // parts
    slots = plane * lines * cap
    lanes = 128
    vmem = pl.BlockSpec(memory_space=pltpu.VMEM)
    dma = pltpu.SemaphoreType.DMA
    returned, back, gd, gu = pl.pallas_call(
        lines_kernel,
        out_shape=(
            jax.ShapeDtypeStruct((parts, plane, lines, cap, wide), bf16),
            jax.ShapeDtypeStruct((tok, slots), bf16),
            jax.ShapeDtypeStruct((rank_dim, width), f32),
            jax.ShapeDtypeStruct((rank_dim, out_width), f32),
        ),
        in_specs=[vmem] * 6,
        out_specs=(pl.BlockSpec(memory_space=pl.ANY),) + (vmem,) * 3,
        scratch_shapes=[
            pltpu.VMEM((chunks, plane, lines, cap, part), bf16),
            pltpu.VMEM((plane, lines, cap, out_width), bf16),
            pltpu.VMEM((chunks, lines, plane, cap, part), bf16),
            pltpu.VMEM((lines, plane, cap, out_width), bf16),
            pltpu.VMEM((parts, lines, 2 * rank_dim, wide), bf16),
            pltpu.VMEM((lines, rank_dim, out_width), bf16),
            pltpu.VMEM((lines, rows, lanes), bf16),
            pltpu.VMEM((lines, rank_dim, lanes), bf16),
            pltpu.VMEM((lines, rows, lanes), bf16),
            pltpu.VMEM((parts, lines, plane, cap, wide), bf16),
            pltpu.VMEM((parts, plane, lines, cap, wide), bf16),
        ]
        + [pltpu.VMEM((chunks, lines, rank_dim, part), bf16)] * 4
        + [pltpu.VMEM((lines, rank_dim, out_width), bf16)] * 4
        + [
            pltpu.VMEM((lines, rank_dim, out_width), f32),
            dma((chunks, plane - 1)), dma((chunks, plane - 1)),
            dma((plane - 1,)), dma((plane - 1,)),
            dma((parts, 2, lines)), dma((parts, lines)),
            dma((2, lines)), dma((lines,)),
            dma((parts, lines)), dma((parts, lines)),
            dma, dma,
            dma((parts, lines, plane - 1)), dma((parts, lines, plane - 1)),
            dma((chunks, 2, lines)), dma((chunks, 2, lines)),
            dma((2, lines)), dma((2, lines)),
            dma((parts,)),
        ],
        compiler_params=pltpu.CompilerParams(
            collective_id=0, has_side_effects=True, vmem_limit_bytes=56 * 1024 * 1024
        ),
        name="adapter_lines",
    )(
        x,
        g,
        tenant.reshape(1, tok),
        adapter_owner_index.reshape(1, -1),
        adapter_down_weight[0, 0].T,
        adapter_up_weight[0, 0],
    )
    tiles = 4
    tile, each = width // tiles, tiles // parts
    columns = lambda c: (0, c)
    down_spec = pl.BlockSpec((rank_dim, tile), columns)
    up_spec = pl.BlockSpec((rank_dim, out_width // tiles), columns)
    passed, gd, gu = pl.pallas_call(
        select_kernel,
        grid=(tiles,),
        out_shape=(
            jax.ShapeDtypeStruct((tok, width), bf16),
            jax.ShapeDtypeStruct((rank_dim, width), f32),
            jax.ShapeDtypeStruct((rank_dim, out_width), f32),
        ),
        in_specs=[
            pl.BlockSpec((1, slots, tile), lambda c: (c // each, 0, c % each)),
            pl.BlockSpec((tok, slots), lambda c: (0, 0)),
            down_spec,
            up_spec,
        ],
        out_specs=(pl.BlockSpec((tok, tile), columns), down_spec, up_spec),
        compiler_params=pltpu.CompilerParams(vmem_limit_bytes=56 * 1024 * 1024),
        name="select_rows",
    )(returned.reshape(parts, slots, wide), back, gd, gu)
    return (passed[None], gd.T[None, None], gu[None, None])


def solution(mesh):
    planned = mesh.shape["segment"] == 2 and mesh.shape["owner"] == lines * plane
    return jax.shard_map(
        local_lines if planned else local,
        mesh=mesh,
        in_specs=(
            P("segment", "owner", None),
            P("segment", "owner", None),
            P("owner", None),
            P(),
            P("segment", "owner", None, None),
            P("segment", "owner", None, None),
        ),
        out_specs=(
            P("segment", "owner", None),
            P("segment", "owner", None, None),
            P("segment", "owner", None, None),
        ),
        check_vma=False,
    )
```

```python
import functools

import jax
import jax.numpy as jnp
from jax import lax
from jax.experimental import pallas as pl
from jax.experimental.pallas import tpu as pltpu
from jax.sharding import PartitionSpec as P

adapter_scale = 2.0


def prefix(x, axis, join, neutral):
    count = lax.axis_size(axis)
    place = lax.axis_index(axis)
    ahead = count - 1 - place
    gathered = lax.all_gather(x.astype(jnp.bfloat16), axis)
    state = jnp.zeros_like(x) + jnp.asarray(neutral, x.dtype)

    def one(step, state):
        source = count - 1 - step
        return join(state, lax.dynamic_index_in_dim(gathered, source, 0, False).astype(x.dtype))

    return lax.fori_loop(0, ahead, one, state)


def local(
    layer_input_rows,
    output_gradient,
    tenant,
    adapter_owner_index,
    adapter_down_weight,
    adapter_up_weight,
):
    inputs = layer_input_rows[0]
    gradient_list = output_gradient[0]
    tok_rows = inputs.shape[0]
    width = inputs.shape[1]
    out_width = gradient_list.shape[1]
    owners = lax.axis_size("owner")
    capacity = 2 * tok_rows // owners
    highest_precision = lax.Precision.HIGHEST
    ids = tenant[:, 0]
    adapter_count = adapter_owner_index.shape[0]
    matched = ids[:, None] == jnp.arange(adapter_count, dtype=jnp.int32)[None, :]
    dest = jnp.sum(jnp.where(matched, adapter_owner_index[None, :], 0), axis=1)
    onehot = (dest[:, None] == jnp.arange(owners, dtype=jnp.int32)[None, :]).astype(jnp.int32)
    rank = jnp.sum((jnp.cumsum(onehot, axis=0) - 1) * onehot, axis=1)
    target = dest * capacity + rank
    placing = (jnp.arange(owners * capacity, dtype=jnp.int32)[:, None] == target[None, :]).astype(
        jnp.bfloat16
    )
    send_inputs = jnp.dot(placing, inputs, preferred_element_type=jnp.float32).astype(jnp.bfloat16)
    send_grads = jnp.dot(placing, gradient_list, preferred_element_type=jnp.float32).astype(
        jnp.bfloat16
    )
    send_inputs = send_inputs.reshape(owners, capacity, width)
    send_grads = send_grads.reshape(owners, capacity, out_width)
    down_factor = adapter_down_weight[0, 0]
    up_factor = adapter_up_weight[0, 0]
    recv_inputs, recv_grads = (
        lax.all_to_all(send_inputs, "owner", split_axis=0, concat_axis=0, tiled=True),
        lax.all_to_all(send_grads, "owner", split_axis=0, concat_axis=0, tiled=True),
    )
    rows_in = recv_inputs.reshape(owners * capacity, width)
    rows_grad = recv_grads.reshape(owners * capacity, out_width)
    scale_weight = adapter_scale * jnp.einsum(
        "rm,km->rk", rows_grad, up_factor, preferred_element_type=jnp.float32
    )
    partial_terms = jnp.einsum(
        "rk,dk->rd",
        scale_weight,
        down_factor,
        precision=highest_precision,
        preferred_element_type=jnp.float32,
    )
    partial_terms = partial_terms.astype(jnp.bfloat16).reshape(owners, capacity, width)
    returned = lax.all_to_all(partial_terms, "owner", split_axis=0, concat_axis=0, tiled=True)
    projected_rows = jnp.dot(rows_in, down_factor, preferred_element_type=jnp.float32)
    grad_down = jnp.einsum(
        "rd,rk->dk",
        rows_in,
        scale_weight,
        precision=highest_precision,
        preferred_element_type=jnp.float32,
    )
    grad_up = jnp.einsum(
        "rk,rm->km",
        projected_rows,
        rows_grad,
        precision=highest_precision,
        preferred_element_type=jnp.float32,
    )
    own_term = jnp.einsum(
        "sr,sd->rd",
        placing,
        returned.reshape(owners * capacity, width),
        preferred_element_type=jnp.float32,
    )

    def combine(earlier, later):
        return earlier + later

    above = prefix(own_term, "segment", combine, jnp.zeros_like(own_term))
    passed = (above + own_term).astype(jnp.bfloat16)
    return (passed[None], grad_down[None, None], grad_up[None, None])


lines = 4
plane = 4
chunks = 4
parts = 2
bf16 = jnp.bfloat16
f32 = jnp.float32


def dot_nt(a, b):
    return lax.dot_general(a, b, (((1,), (1,)), ((), ())), preferred_element_type=f32)


def dot_nn(a, b):
    return jnp.dot(a, b, preferred_element_type=f32)


def lines_kernel(
    x, g, ids, owner_of, a, b,
    returned, back, gd, gu,
    sx, sg, rx, rg, at, cfo, cfto, cf, cft, c1, ts, tr, sl, sr, ql, qr, pjs, pjr,
    x_s, x_r, g_s, g_r, a_s, a_r, a1_s, a1_r, c_s, c_r, t_s, t_r, d_s, d_r, f_s, f_r, p_s, p_r, o_s,
):
    tok, width = x.shape
    out_width = g.shape[1]
    part = width // chunks
    wide = width // parts
    cap = sx.shape[3]
    rank_dim = b.shape[0]
    rows = plane * cap
    seg = lax.axis_index("segment")
    own = lax.axis_index("owner")
    z = own // plane
    h = own % plane
    upper = seg == 1
    lower = seg == 0
    pending = []

    def signal(segment, owner):
        pl.semaphore_signal(
            barrier, inc=1, device_id=(segment, owner), device_id_type=pl.DeviceIdType.MESH
        )

    def copy(source, sink, send, recv, segment, owner):
        return pltpu.make_async_remote_copy(
            src_ref=source, dst_ref=sink, send_sem=send, recv_sem=recv,
            device_id=(segment, owner), device_id_type=pl.DeviceIdType.MESH,
        )

    def go(cond, make):
        if cond is None:
            make().start()
        else:
            pl.when(cond)(lambda: make().start())
        pending.append((cond, make))

    def host(k):
        return z * plane + (h + k) % plane

    has_left = z > 0
    has_right = z < lines - 1

    barrier = pltpu.get_barrier_semaphore()
    for k in range(1, lines * plane):
        signal(seg, (own + k) % (lines * plane))
    signal(1 - seg, own)

    n_owner = lines * plane
    n_adapter = owner_of.shape[1]
    square = (n_adapter, n_adapter)
    diagonal = lax.broadcasted_iota(jnp.int32, square, 0) == lax.broadcasted_iota(jnp.int32, square, 1)
    owner_column = jnp.sum(jnp.where(diagonal, owner_of[...], 0), axis=1, keepdims=True)
    matched = lax.broadcasted_iota(jnp.int32, (n_adapter, tok), 0) == ids[...]
    dest = jnp.sum(jnp.where(matched, owner_column, 0), axis=0, keepdims=True)
    onehot = (lax.broadcasted_iota(jnp.int32, (n_owner, tok), 0) == dest).astype(f32)
    earlier = (
        lax.broadcasted_iota(jnp.int32, (tok, tok), 0)
        < lax.broadcasted_iota(jnp.int32, (tok, tok), 1)
    ).astype(f32)
    count = dot_nn(onehot.astype(bf16), earlier.astype(bf16))
    rank = jnp.sum(count * onehot, axis=0, keepdims=True).astype(jnp.int32)
    target = (dest % plane) * (lines * cap) + (dest // plane) * cap + rank
    placing32 = (
        lax.broadcasted_iota(jnp.int32, (plane * lines * cap, tok), 0) == target
    ).astype(f32)
    placing = placing32.astype(bf16)
    back[...] = placing32.T.astype(bf16)

    for p in range(parts):
        at[p, z, :rank_dim] = a[:, p * wide : (p + 1) * wide]
    sg[...] = dot_nn(placing, g[...]).astype(bf16).reshape(plane, lines, cap, out_width)
    pl.semaphore_wait(barrier, lines * plane)

    def shard_right(view, send, recv, k):
        ref = view(z - k)
        return copy(ref, ref, send.at[0, k], recv.at[z - k], seg, own + plane)

    def shard_left(view, send, recv, k):
        ref = view(z + k)
        return copy(ref, ref, send.at[1, k], recv.at[z + k], seg, own - plane)

    def shard_go(view, send, recv, k):
        go((z >= k) & has_right, lambda: shard_right(view, send, recv, k))
        go((z + k < lines) & has_left, lambda: shard_left(view, send, recv, k))

    def shard_wait(view, send, recv, k):
        pl.when(z >= k)(lambda: shard_right(view, send, recv, k).wait_recv())
        pl.when(z + k < lines)(lambda: shard_left(view, send, recv, k).wait_recv())

    def a_view(p):
        return lambda j: at.at[p, j, pl.ds(0, rank_dim)]

    def across(p, j):
        return copy(
            at.at[p, j, pl.ds(0, rank_dim)], at.at[p, j, pl.ds(rank_dim, rank_dim)],
            a1_s.at[p, j], a1_r.at[p, j], 0, own,
        )

    def a_start(p):
        shard_go(a_view(p), a_s.at[p], a_r.at[p], 0)

    def a_step(k, p):
        shard_wait(a_view(p), a_s.at[p], a_r.at[p], k)
        if k < lines - 1:
            shard_go(a_view(p), a_s.at[p], a_r.at[p], k)
        go((z >= k) & upper, lambda: across(p, z - k))
        go((z + k < lines) & upper, lambda: across(p, z + k))

    pairs = [(d, k) for d in range(lines) for k in range(plane) if d + k > 0]

    def g_copy(d, k):
        goal, place = (z + d) % lines, (h + k) % plane
        return copy(
            sg.at[place, goal], rg.at[z, h], g_s.at[d, k], g_r.at[d, k], seg, goal * plane + place
        )

    def x_copy(q, k):
        return copy(
            sx.at[q, (h + k) % plane], rx.at[q, :, h], x_s.at[q, k - 1], x_r.at[q, k - 1], seg, host(k)
        )

    for d, k in pairs:
        go(None, functools.partial(g_copy, d, k))
    rg[z, h] = sg[h, z]
    for p in range(parts):
        go(upper, functools.partial(across, p, z))
    for q in range(chunks):
        sx[q] = (
            dot_nn(placing, x[:, q * part : (q + 1) * part])
            .astype(bf16)
            .reshape(plane, lines, cap, part)
        )
        for k in range(1, plane):
            go(None, functools.partial(x_copy, q, k))
        rx[q, :, h] = sx[q, h]
    a_start(0)

    cfo[...] = jnp.zeros_like(cfo)
    cfto[...] = jnp.zeros_like(cfto)
    pjs[...] = jnp.zeros_like(pjs)
    for d, k in pairs:
        g_copy(d, k).wait_recv()
    for j in range(lines):
        grads = rg[j].reshape(rows, out_width)
        cfto[j, :, :rows] = (adapter_scale * dot_nt(b[...], grads)).astype(bf16)
        cfo[j, :, :rank_dim] = (adapter_scale * dot_nt(grads, b[...])).astype(bf16)

    def coef_back(d, which):
        goal = (z + d) % lines
        source, sink = ((cfto, cft), (cfo, cf))[which]
        return copy(
            source.at[goal], sink.at[z], f_s.at[which, d], f_r.at[which, d], seg, goal * plane + h
        )

    for which in range(2):
        for d in range(1, lines):
            go(None, functools.partial(coef_back, d, which))
    cft[z] = cfto[z]
    cf[z] = cfo[z]
    a_start(1)
    for d in range(1, lines):
        coef_back(d, 0).wait_recv()

    def coef_copy():
        return copy(cf, c1, c_s, c_r, 0, own)

    def sums(value, cols, send_l, send_r, recv_l, recv_r, s_sem, r_sem):
        def left(t):
            return copy(send_l.at[t], recv_l.at[t], s_sem.at[0, t], r_sem.at[0, t], seg, own - plane)

        def right(t):
            return copy(send_r.at[t], recv_r.at[t], s_sem.at[1, t], r_sem.at[1, t], seg, own + plane)

        def hop(stage):
            for t in range(lines - 1 - stage):
                for goal, buf, got, make, cond in (
                    (t, send_l, recv_l, left, z == lines - 1 - stage),
                    (lines - 1 - t, send_r, recv_r, right, z == stage),
                ):
                    @pl.when(cond)
                    def _():
                        mine = value(goal)
                        if stage > 0:
                            make(goal).wait_recv()
                            mine += got[goal].astype(f32)
                        buf[goal] = mine.astype(bf16)

                    go(cond, functools.partial(make, goal))

        def finish(out):
            out[:, cols] = value(z)

            @pl.when(has_right)
            def _():
                left(z).wait_recv()
                out[:, cols] += recv_l[z].astype(f32)

            @pl.when(has_left)
            def _():
                right(z).wait_recv()
                out[:, cols] += recv_r[z].astype(f32)

        return hop, finish

    downs = [
        sums(
            lambda j, q=q: dot_nn(cft[j, :, :rows], rx[q, j].reshape(rows, part)),
            pl.ds(q * part, part),
            sl.at[q], sr.at[q], ql.at[q], qr.at[q], d_s.at[q], d_r.at[q],
        )
        for q in range(chunks)
    ]

    def down_hop(q, stage):
        if stage == 0:
            for k in range(1, plane):
                x_copy(q, k).wait_recv()
        downs[q][0](stage)

    order = (z, z + 1 - 2 * (z % 2), 2 - z // 2, 3 - 3 * (z // 2))

    def t_copy(p, i, k):
        return copy(
            ts.at[p, order[i], (h + k) % plane], tr.at[p, h, order[i]],
            t_s.at[p, i, k - 1], t_r.at[p, i, k - 1], seg, host(k),
        )

    def term(i, p):
        j = order[i]

        @pl.when(upper)
        def _():
            total = dot_nn(cf[j, :, :rank_dim], at[p, j, :rank_dim])
            ts[p, j] = total.astype(bf16).reshape(plane, cap, wide)

        @pl.when(lower)
        def _():
            across(p, j).wait_recv()
            total = dot_nn(cf[j, :, : 2 * rank_dim], at[p, j])
            ts[p, j] = total.astype(bf16).reshape(plane, cap, wide)

        for k in range(1, plane):
            go(None, functools.partial(t_copy, p, i, k))
        tr[p, h, j] = ts[p, j, h]

    def project(i):
        j = order[i]
        proj = jnp.zeros((rank_dim, rows), f32)
        for q in range(chunks):
            p, first = q * part // wide, q * part % wide
            proj += dot_nt(at[p, j, :rank_dim, first : first + part], rx[q, j].reshape(rows, part))
        if i == 0:
            pjr[z, :, :rows] = proj.astype(bf16)
        else:
            pjs[j, :, :rows] = proj.astype(bf16)
            go(None, lambda: copy(pjs.at[j], pjr.at[z], p_s.at[i], p_r.at[z], seg, j * plane + h))

    down_hop(0, 0)
    for d in range(1, lines):
        coef_back(d, 1).wait_recv()
    go(upper, coef_copy)
    down_hop(1, 0)
    a_step(1, 0)
    a_step(1, 1)
    down_hop(2, 0)
    down_hop(0, 1)
    a_step(2, 0)
    down_hop(3, 0)
    a_step(2, 1)

    @pl.when(lower)
    def _():
        coef_copy().wait_recv()
        cf[:, :, rank_dim : 2 * rank_dim] = c1[:, :, :rank_dim]

    term(0, 0)
    term(0, 1)
    down_hop(1, 1)
    down_hop(0, 2)
    term(1, 0)
    term(1, 1)
    down_hop(2, 1)
    down_hop(1, 2)
    term(2, 0)
    term(2, 1)
    project(0)
    project(1)
    a_step(3, 0)
    a_step(3, 1)
    project(2)
    project(3)
    down_hop(3, 1)
    down_hop(2, 2)
    term(3, 0)
    down_hop(3, 2)
    term(3, 1)
    for _, finish in downs:
        finish(gd)
    for d in range(1, lines):
        other = (z + d) % lines
        copy(pjs.at[other], pjr.at[other], p_s.at[d], p_r.at[other], seg, host(1)).wait_recv()
    gu[...] = sum(
        dot_nn(pjr[j, :, :rows], rg[j].reshape(rows, out_width)) for j in range(lines)
    )
    for p in range(parts):
        for i in range(lines):
            for k in range(1, plane):
                t_copy(p, i, k).wait_recv()
        pltpu.make_async_copy(tr.at[p], returned.at[p], o_s.at[p]).start()
    for p in range(parts):
        pltpu.make_async_copy(tr.at[p], returned.at[p], o_s.at[p]).wait()
    for cond, make in pending:
        if cond is None:
            make().wait_send()
        else:
            pl.when(cond)(functools.partial(lambda make: make().wait_send(), make))


def select_kernel(returned, back, gd_in, gu_in, passed, gd, gu):
    passed[...] = dot_nn(back[...], returned[0]).astype(bf16)
    gd[...] = gd_in[...]
    gu[...] = gu_in[...]


def local_lines(
    layer_input_rows,
    output_gradient,
    tenant,
    adapter_owner_index,
    adapter_down_weight,
    adapter_up_weight,
):
    x, g = layer_input_rows[0], output_gradient[0]
    tok, width = x.shape
    out_width = g.shape[1]
    rank_dim = adapter_up_weight.shape[2]
    cap = 2 * tok // (lines * plane)
    rows = plane * cap
    part = width // chunks
    wide = width // parts
    slots = plane * lines * cap
    lanes = 128
    vmem = pl.BlockSpec(memory_space=pltpu.VMEM)
    dma = pltpu.SemaphoreType.DMA
    returned, back, gd, gu = pl.pallas_call(
        lines_kernel,
        out_shape=(
            jax.ShapeDtypeStruct((parts, plane, lines, cap, wide), bf16),
            jax.ShapeDtypeStruct((tok, slots), bf16),
            jax.ShapeDtypeStruct((rank_dim, width), f32),
            jax.ShapeDtypeStruct((rank_dim, out_width), f32),
        ),
        in_specs=[vmem] * 6,
        out_specs=(pl.BlockSpec(memory_space=pl.ANY),) + (vmem,) * 3,
        scratch_shapes=[
            pltpu.VMEM((chunks, plane, lines, cap, part), bf16),
            pltpu.VMEM((plane, lines, cap, out_width), bf16),
            pltpu.VMEM((chunks, lines, plane, cap, part), bf16),
            pltpu.VMEM((lines, plane, cap, out_width), bf16),
            pltpu.VMEM((parts, lines, 2 * rank_dim, wide), bf16),
            pltpu.VMEM((lines, rows, lanes), bf16),
            pltpu.VMEM((lines, rank_dim, lanes), bf16),
            pltpu.VMEM((lines, rows, lanes), bf16),
            pltpu.VMEM((lines, rank_dim, lanes), bf16),
            pltpu.VMEM((lines, rows, lanes), bf16),
            pltpu.VMEM((parts, lines, plane, cap, wide), bf16),
            pltpu.VMEM((parts, plane, lines, cap, wide), bf16),
        ]
        + [pltpu.VMEM((chunks, lines, rank_dim, part), bf16)] * 4
        + [pltpu.VMEM((lines, rank_dim, lanes), bf16)] * 2
        + [
            dma((chunks, plane - 1)), dma((chunks, plane - 1)),
            dma((lines, plane)), dma((lines, plane)),
            dma((parts, 2, lines)), dma((parts, lines)),
            dma((parts, lines)), dma((parts, lines)),
            dma, dma,
            dma((parts, lines, plane - 1)), dma((parts, lines, plane - 1)),
            dma((chunks, 2, lines)), dma((chunks, 2, lines)),
            dma((2, lines)), dma((2, lines)),
            dma((lines,)), dma((lines,)),
            dma((parts,)),
        ],
        compiler_params=pltpu.CompilerParams(
            collective_id=0, has_side_effects=True, vmem_limit_bytes=56 * 1024 * 1024
        ),
        name="adapter_lines",
    )(
        x,
        g,
        tenant.reshape(1, tok),
        adapter_owner_index.reshape(1, -1),
        adapter_down_weight[0, 0].T,
        adapter_up_weight[0, 0],
    )
    tiles = 4
    tile, each = width // tiles, tiles // parts
    columns = lambda c: (0, c)
    down_spec = pl.BlockSpec((rank_dim, tile), columns)
    up_spec = pl.BlockSpec((rank_dim, out_width // tiles), columns)
    passed, gd, gu = pl.pallas_call(
        select_kernel,
        grid=(tiles,),
        out_shape=(
            jax.ShapeDtypeStruct((tok, width), bf16),
            jax.ShapeDtypeStruct((rank_dim, width), f32),
            jax.ShapeDtypeStruct((rank_dim, out_width), f32),
        ),
        in_specs=[
            pl.BlockSpec((1, slots, tile), lambda c: (c // each, 0, c % each)),
            pl.BlockSpec((tok, slots), lambda c: (0, 0)),
            down_spec,
            up_spec,
        ],
        out_specs=(pl.BlockSpec((tok, tile), columns), down_spec, up_spec),
        compiler_params=pltpu.CompilerParams(vmem_limit_bytes=56 * 1024 * 1024),
        name="select_rows",
    )(returned.reshape(parts, slots, wide), back, gd, gu)
    return (passed[None], gd.T[None, None], gu[None, None])


def solution(mesh):
    planned = mesh.shape["segment"] == 2 and mesh.shape["owner"] == lines * plane
    return jax.shard_map(
        local_lines if planned else local,
        mesh=mesh,
        in_specs=(
            P("segment", "owner", None),
            P("segment", "owner", None),
            P("owner", None),
            P(),
            P("segment", "owner", None, None),
            P("segment", "owner", None, None),
        ),
        out_specs=(
            P("segment", "owner", None),
            P("segment", "owner", None, None),
            P("segment", "owner", None, None),
        ),
        check_vma=False,
    )
```

```python
import functools

import jax
import jax.numpy as jnp
from jax import lax
from jax.experimental import pallas as pl
from jax.experimental.pallas import tpu as pltpu
from jax.sharding import PartitionSpec as P

adapter_scale = 2.0


def prefix(x, axis, join, neutral):
    count = lax.axis_size(axis)
    place = lax.axis_index(axis)
    ahead = count - 1 - place
    gathered = lax.all_gather(x.astype(jnp.bfloat16), axis)
    state = jnp.zeros_like(x) + jnp.asarray(neutral, x.dtype)

    def one(step, state):
        source = count - 1 - step
        return join(state, lax.dynamic_index_in_dim(gathered, source, 0, False).astype(x.dtype))

    return lax.fori_loop(0, ahead, one, state)


def local(
    layer_input_rows,
    output_gradient,
    tenant,
    adapter_owner_index,
    adapter_down_weight,
    adapter_up_weight,
):
    inputs = layer_input_rows[0]
    gradient_list = output_gradient[0]
    tok_rows = inputs.shape[0]
    width = inputs.shape[1]
    out_width = gradient_list.shape[1]
    owners = lax.axis_size("owner")
    capacity = 2 * tok_rows // owners
    highest_precision = lax.Precision.HIGHEST
    ids = tenant[:, 0]
    adapter_count = adapter_owner_index.shape[0]
    matched = ids[:, None] == jnp.arange(adapter_count, dtype=jnp.int32)[None, :]
    dest = jnp.sum(jnp.where(matched, adapter_owner_index[None, :], 0), axis=1)
    onehot = (dest[:, None] == jnp.arange(owners, dtype=jnp.int32)[None, :]).astype(jnp.int32)
    rank = jnp.sum((jnp.cumsum(onehot, axis=0) - 1) * onehot, axis=1)
    target = dest * capacity + rank
    placing = (jnp.arange(owners * capacity, dtype=jnp.int32)[:, None] == target[None, :]).astype(
        jnp.bfloat16
    )
    send_inputs = jnp.dot(placing, inputs, preferred_element_type=jnp.float32).astype(jnp.bfloat16)
    send_grads = jnp.dot(placing, gradient_list, preferred_element_type=jnp.float32).astype(
        jnp.bfloat16
    )
    send_inputs = send_inputs.reshape(owners, capacity, width)
    send_grads = send_grads.reshape(owners, capacity, out_width)
    down_factor = adapter_down_weight[0, 0]
    up_factor = adapter_up_weight[0, 0]
    recv_inputs, recv_grads = (
        lax.all_to_all(send_inputs, "owner", split_axis=0, concat_axis=0, tiled=True),
        lax.all_to_all(send_grads, "owner", split_axis=0, concat_axis=0, tiled=True),
    )
    rows_in = recv_inputs.reshape(owners * capacity, width)
    rows_grad = recv_grads.reshape(owners * capacity, out_width)
    scale_weight = adapter_scale * jnp.einsum(
        "rm,km->rk", rows_grad, up_factor, preferred_element_type=jnp.float32
    )
    partial_terms = jnp.einsum(
        "rk,dk->rd",
        scale_weight,
        down_factor,
        precision=highest_precision,
        preferred_element_type=jnp.float32,
    )
    partial_terms = partial_terms.astype(jnp.bfloat16).reshape(owners, capacity, width)
    returned = lax.all_to_all(partial_terms, "owner", split_axis=0, concat_axis=0, tiled=True)
    projected_rows = jnp.dot(rows_in, down_factor, preferred_element_type=jnp.float32)
    grad_down = jnp.einsum(
        "rd,rk->dk",
        rows_in,
        scale_weight,
        precision=highest_precision,
        preferred_element_type=jnp.float32,
    )
    grad_up = jnp.einsum(
        "rk,rm->km",
        projected_rows,
        rows_grad,
        precision=highest_precision,
        preferred_element_type=jnp.float32,
    )
    own_term = jnp.einsum(
        "sr,sd->rd",
        placing,
        returned.reshape(owners * capacity, width),
        preferred_element_type=jnp.float32,
    )

    def combine(earlier, later):
        return earlier + later

    above = prefix(own_term, "segment", combine, jnp.zeros_like(own_term))
    passed = (above + own_term).astype(jnp.bfloat16)
    return (passed[None], grad_down[None, None], grad_up[None, None])


lines = 4
plane = 4
chunks = 4
parts = 2
bf16 = jnp.bfloat16
f32 = jnp.float32


def dot_nt(a, b):
    return lax.dot_general(a, b, (((1,), (1,)), ((), ())), preferred_element_type=f32)


def dot_nn(a, b):
    return jnp.dot(a, b, preferred_element_type=f32)


def lines_kernel(
    x, g, ids, owner_of, a, b,
    returned, back, gd, gu,
    sx, sg, rx, rg, at, cfo, cfto, cf, cft, c1, ts, tr, sl, sr, ql, qr, pjs, pjr,
    x_s, x_r, g_s, g_r, a_s, a_r, a1_s, a1_r, c_s, c_r, t_s, t_r, d_s, d_r, f_s, f_r, p_s, p_r, o_s,
):
    tok, width = x.shape
    out_width = g.shape[1]
    part = width // chunks
    wide = width // parts
    cap = sx.shape[3]
    rank_dim = b.shape[0]
    rows = plane * cap
    seg = lax.axis_index("segment")
    own = lax.axis_index("owner")
    z = own // plane
    h = own % plane
    upper = seg == 1
    lower = seg == 0
    pending = []

    def signal(segment, owner):
        pl.semaphore_signal(
            barrier, inc=1, device_id=(segment, owner), device_id_type=pl.DeviceIdType.MESH
        )

    def copy(source, sink, send, recv, segment, owner):
        return pltpu.make_async_remote_copy(
            src_ref=source, dst_ref=sink, send_sem=send, recv_sem=recv,
            device_id=(segment, owner), device_id_type=pl.DeviceIdType.MESH,
        )

    def go(cond, make):
        if cond is None:
            make().start()
        else:
            pl.when(cond)(lambda: make().start())
        pending.append((cond, make))

    def host(k):
        return z * plane + (h + k) % plane

    has_left = z > 0
    has_right = z < lines - 1

    barrier = pltpu.get_barrier_semaphore()
    for k in range(1, lines * plane):
        signal(seg, (own + k) % (lines * plane))
    signal(1 - seg, own)

    n_owner = lines * plane
    n_adapter = owner_of.shape[1]
    square = (n_adapter, n_adapter)
    diagonal = lax.broadcasted_iota(jnp.int32, square, 0) == lax.broadcasted_iota(jnp.int32, square, 1)
    owner_column = jnp.sum(jnp.where(diagonal, owner_of[...], 0), axis=1, keepdims=True)
    matched = lax.broadcasted_iota(jnp.int32, (n_adapter, tok), 0) == ids[...]
    dest = jnp.sum(jnp.where(matched, owner_column, 0), axis=0, keepdims=True)
    onehot = (lax.broadcasted_iota(jnp.int32, (n_owner, tok), 0) == dest).astype(f32)
    earlier = (
        lax.broadcasted_iota(jnp.int32, (tok, tok), 0)
        < lax.broadcasted_iota(jnp.int32, (tok, tok), 1)
    ).astype(f32)
    count = dot_nn(onehot.astype(bf16), earlier.astype(bf16))
    rank = jnp.sum(count * onehot, axis=0, keepdims=True).astype(jnp.int32)
    target = (dest % plane) * (lines * cap) + (dest // plane) * cap + rank
    placing32 = (
        lax.broadcasted_iota(jnp.int32, (plane * lines * cap, tok), 0) == target
    ).astype(f32)
    placing = placing32.astype(bf16)
    back[...] = placing32.T.astype(bf16)

    for p in range(parts):
        at[p, z, :rank_dim] = a[:, p * wide : (p + 1) * wide]
    sg[...] = dot_nn(placing, g[...]).astype(bf16).reshape(plane, lines, cap, out_width)
    pl.semaphore_wait(barrier, lines * plane)

    def shard_right(view, send, recv, k):
        ref = view(z - k)
        return copy(ref, ref, send.at[0, k], recv.at[z - k], seg, own + plane)

    def shard_left(view, send, recv, k):
        ref = view(z + k)
        return copy(ref, ref, send.at[1, k], recv.at[z + k], seg, own - plane)

    def shard_go(view, send, recv, k):
        go((z >= k) & has_right, lambda: shard_right(view, send, recv, k))
        go((z + k < lines) & has_left, lambda: shard_left(view, send, recv, k))

    def shard_wait(view, send, recv, k):
        pl.when(z >= k)(lambda: shard_right(view, send, recv, k).wait_recv())
        pl.when(z + k < lines)(lambda: shard_left(view, send, recv, k).wait_recv())

    def a_view(p):
        return lambda j: at.at[p, j, pl.ds(0, rank_dim)]

    def across(p, j):
        return copy(
            at.at[p, j, pl.ds(0, rank_dim)], at.at[p, j, pl.ds(rank_dim, rank_dim)],
            a1_s.at[p, j], a1_r.at[p, j], 0, own,
        )

    def a_start(p):
        shard_go(a_view(p), a_s.at[p], a_r.at[p], 0)

    def a_step(k, p):
        shard_wait(a_view(p), a_s.at[p], a_r.at[p], k)
        if k < lines - 1:
            shard_go(a_view(p), a_s.at[p], a_r.at[p], k)
        go((z >= k) & upper, lambda: across(p, z - k))
        go((z + k < lines) & upper, lambda: across(p, z + k))

    pairs = [(d, k) for d in range(lines) for k in range(plane) if d + k > 0]

    def g_copy(d, k):
        goal, place = (z + d) % lines, (h + k) % plane
        return copy(
            sg.at[place, goal], rg.at[z, h], g_s.at[d, k], g_r.at[d, k], seg, goal * plane + place
        )

    def x_copy(q, k):
        return copy(
            sx.at[q, (h + k) % plane], rx.at[q, :, h], x_s.at[q, k - 1], x_r.at[q, k - 1], seg, host(k)
        )

    for d, k in pairs:
        go(None, functools.partial(g_copy, d, k))
    rg[z, h] = sg[h, z]
    for p in range(parts):
        go(upper, functools.partial(across, p, z))
    for q in range(chunks):
        sx[q] = (
            dot_nn(placing, x[:, q * part : (q + 1) * part])
            .astype(bf16)
            .reshape(plane, lines, cap, part)
        )
        for k in range(1, plane):
            go(None, functools.partial(x_copy, q, k))
        rx[q, :, h] = sx[q, h]
    a_start(0)

    cfo[...] = jnp.zeros_like(cfo)
    cfto[...] = jnp.zeros_like(cfto)
    pjs[...] = jnp.zeros_like(pjs)
    for d, k in pairs:
        g_copy(d, k).wait_recv()
    for j in range(lines):
        grads = rg[j].reshape(rows, out_width)
        cfto[j, :, :rows] = (adapter_scale * dot_nt(b[...], grads)).astype(bf16)
        cfo[j, :, :rank_dim] = (adapter_scale * dot_nt(grads, b[...])).astype(bf16)

    def coef_back(d, which):
        goal = (z + d) % lines
        source, sink = ((cfto, cft), (cfo, cf))[which]
        return copy(
            source.at[goal], sink.at[z], f_s.at[which, d], f_r.at[which, d], seg, goal * plane + h
        )

    for which in range(2):
        for d in range(1, lines):
            go(None, functools.partial(coef_back, d, which))
    cft[z] = cfto[z]
    cf[z] = cfo[z]
    a_start(1)
    for d in range(1, lines):
        coef_back(d, 0).wait_recv()

    def coef_copy():
        return copy(cf, c1, c_s, c_r, 0, own)

    def sums(value, cols, send_l, send_r, recv_l, recv_r, s_sem, r_sem):
        def left(t):
            return copy(send_l.at[t], recv_l.at[t], s_sem.at[0, t], r_sem.at[0, t], seg, own - plane)

        def right(t):
            return copy(send_r.at[t], recv_r.at[t], s_sem.at[1, t], r_sem.at[1, t], seg, own + plane)

        def hop(stage):
            for t in range(lines - 1 - stage):
                for goal, buf, got, make, cond in (
                    (t, send_l, recv_l, left, z == lines - 1 - stage),
                    (lines - 1 - t, send_r, recv_r, right, z == stage),
                ):
                    @pl.when(cond)
                    def _():
                        mine = value(goal)
                        if stage > 0:
                            make(goal).wait_recv()
                            mine += got[goal].astype(f32)
                        buf[goal] = mine.astype(bf16)

                    go(cond, functools.partial(make, goal))

        def finish(out):
            out[:, cols] = value(z)

            @pl.when(has_right)
            def _():
                left(z).wait_recv()
                out[:, cols] += recv_l[z].astype(f32)

            @pl.when(has_left)
            def _():
                right(z).wait_recv()
                out[:, cols] += recv_r[z].astype(f32)

        return hop, finish

    downs = [
        sums(
            lambda j, q=q: dot_nn(cft[j, :, :rows], rx[q, j].reshape(rows, part)),
            pl.ds(q * part, part),
            sl.at[q], sr.at[q], ql.at[q], qr.at[q], d_s.at[q], d_r.at[q],
        )
        for q in range(chunks)
    ]

    def down_hop(q, stage):
        if stage == 0:
            for k in range(1, plane):
                x_copy(q, k).wait_recv()
        downs[q][0](stage)

    order = (z, z + 1 - 2 * (z % 2), 2 - z // 2, 3 - 3 * (z // 2))

    def t_copy(p, i, k):
        return copy(
            ts.at[p, order[i], (h + k) % plane], tr.at[p, h, order[i]],
            t_s.at[p, i, k - 1], t_r.at[p, i, k - 1], seg, host(k),
        )

    def term(i, p):
        j = order[i]

        @pl.when(upper)
        def _():
            total = dot_nn(cf[j, :, :rank_dim], at[p, j, :rank_dim])
            ts[p, j] = total.astype(bf16).reshape(plane, cap, wide)

        @pl.when(lower)
        def _():
            across(p, j).wait_recv()
            total = dot_nn(cf[j, :, : 2 * rank_dim], at[p, j])
            ts[p, j] = total.astype(bf16).reshape(plane, cap, wide)

        for k in range(1, plane):
            go(None, functools.partial(t_copy, p, i, k))
        tr[p, h, j] = ts[p, j, h]

    def project(i):
        j = order[i]
        proj = jnp.zeros((rank_dim, rows), f32)
        for q in range(chunks):
            p, first = q * part // wide, q * part % wide
            proj += dot_nt(at[p, j, :rank_dim, first : first + part], rx[q, j].reshape(rows, part))
        if i == 0:
            pjr[z, :, :rows] = proj.astype(bf16)
        else:
            pjs[j, :, :rows] = proj.astype(bf16)
            go(None, lambda: copy(pjs.at[j], pjr.at[z], p_s.at[i], p_r.at[z], seg, j * plane + h))

    down_hop(0, 0)
    for d in range(1, lines):
        coef_back(d, 1).wait_recv()
    go(upper, coef_copy)
    down_hop(1, 0)
    a_step(1, 0)
    a_step(1, 1)
    down_hop(2, 0)
    down_hop(0, 1)
    a_step(2, 0)
    down_hop(3, 0)
    a_step(2, 1)

    @pl.when(lower)
    def _():
        coef_copy().wait_recv()
        cf[:, :, rank_dim : 2 * rank_dim] = c1[:, :, :rank_dim]

    term(0, 0)
    term(0, 1)
    down_hop(1, 1)
    down_hop(0, 2)
    term(1, 0)
    term(1, 1)
    down_hop(2, 1)
    down_hop(1, 2)
    term(2, 0)
    term(2, 1)
    project(0)
    project(1)
    a_step(3, 0)
    a_step(3, 1)
    project(2)
    project(3)
    down_hop(3, 1)
    down_hop(2, 2)
    term(3, 0)
    down_hop(3, 2)
    term(3, 1)
    for _, finish in downs:
        finish(gd)
    for d in range(1, lines):
        other = (z + d) % lines
        copy(pjs.at[other], pjr.at[other], p_s.at[d], p_r.at[other], seg, host(1)).wait_recv()
    gu[...] = sum(
        dot_nn(pjr[j, :, :rows], rg[j].reshape(rows, out_width)) for j in range(lines)
    )
    for p in range(parts):
        for i in range(lines):
            for k in range(1, plane):
                t_copy(p, i, k).wait_recv()
        pltpu.make_async_copy(tr.at[p], returned.at[p], o_s.at[p]).start()
    for p in range(parts):
        pltpu.make_async_copy(tr.at[p], returned.at[p], o_s.at[p]).wait()
    for cond, make in pending:
        if cond is None:
            make().wait_send()
        else:
            pl.when(cond)(functools.partial(lambda make: make().wait_send(), make))


def select_kernel(returned, back, gd_in, gu_in, passed, gd, gu, sems):
    step = pl.program_id(0)
    moves = [
        pltpu.make_async_copy(gd_in, gd, sems.at[0]),
        pltpu.make_async_copy(gu_in, gu, sems.at[1]),
    ]

    @pl.when(step == 0)
    def _():
        for move in moves:
            move.start()

    passed[...] = dot_nn(back[...], returned[0]).astype(bf16)

    @pl.when(step == pl.num_programs(0) - 1)
    def _():
        for move in moves:
            move.wait()


def local_lines(
    layer_input_rows,
    output_gradient,
    tenant,
    adapter_owner_index,
    adapter_down_weight,
    adapter_up_weight,
):
    x, g = layer_input_rows[0], output_gradient[0]
    tok, width = x.shape
    out_width = g.shape[1]
    rank_dim = adapter_up_weight.shape[2]
    cap = 2 * tok // (lines * plane)
    rows = plane * cap
    part = width // chunks
    wide = width // parts
    slots = plane * lines * cap
    lanes = 128
    vmem = pl.BlockSpec(memory_space=pltpu.VMEM)
    dma = pltpu.SemaphoreType.DMA
    returned, back, gd, gu = pl.pallas_call(
        lines_kernel,
        out_shape=(
            jax.ShapeDtypeStruct((parts, plane, lines, cap, wide), bf16),
            jax.ShapeDtypeStruct((tok, slots), bf16),
            jax.ShapeDtypeStruct((rank_dim, width), f32),
            jax.ShapeDtypeStruct((rank_dim, out_width), f32),
        ),
        in_specs=[vmem] * 6,
        out_specs=(pl.BlockSpec(memory_space=pl.ANY),) + (vmem,) * 3,
        scratch_shapes=[
            pltpu.VMEM((chunks, plane, lines, cap, part), bf16),
            pltpu.VMEM((plane, lines, cap, out_width), bf16),
            pltpu.VMEM((chunks, lines, plane, cap, part), bf16),
            pltpu.VMEM((lines, plane, cap, out_width), bf16),
            pltpu.VMEM((parts, lines, 2 * rank_dim, wide), bf16),
            pltpu.VMEM((lines, rows, lanes), bf16),
            pltpu.VMEM((lines, rank_dim, lanes), bf16),
            pltpu.VMEM((lines, rows, lanes), bf16),
            pltpu.VMEM((lines, rank_dim, lanes), bf16),
            pltpu.VMEM((lines, rows, lanes), bf16),
            pltpu.VMEM((parts, lines, plane, cap, wide), bf16),
            pltpu.VMEM((parts, plane, lines, cap, wide), bf16),
        ]
        + [pltpu.VMEM((chunks, lines, rank_dim, part), bf16)] * 4
        + [pltpu.VMEM((lines, rank_dim, lanes), bf16)] * 2
        + [
            dma((chunks, plane - 1)), dma((chunks, plane - 1)),
            dma((lines, plane)), dma((lines, plane)),
            dma((parts, 2, lines)), dma((parts, lines)),
            dma((parts, lines)), dma((parts, lines)),
            dma, dma,
            dma((parts, lines, plane - 1)), dma((parts, lines, plane - 1)),
            dma((chunks, 2, lines)), dma((chunks, 2, lines)),
            dma((2, lines)), dma((2, lines)),
            dma((lines,)), dma((lines,)),
            dma((parts,)),
        ],
        compiler_params=pltpu.CompilerParams(
            collective_id=0, has_side_effects=True, vmem_limit_bytes=56 * 1024 * 1024
        ),
        name="adapter_lines",
    )(
        x,
        g,
        tenant.reshape(1, tok),
        adapter_owner_index.reshape(1, -1),
        adapter_down_weight[0, 0].T,
        adapter_up_weight[0, 0],
    )
    tiles = 4
    tile, each = width // tiles, tiles // parts
    columns = lambda c: (0, c)
    whole = pl.BlockSpec(memory_space=pl.ANY)
    passed, gd, gu = pl.pallas_call(
        select_kernel,
        grid=(tiles,),
        out_shape=(
            jax.ShapeDtypeStruct((tok, width), bf16),
            jax.ShapeDtypeStruct((rank_dim, width), f32),
            jax.ShapeDtypeStruct((rank_dim, out_width), f32),
        ),
        in_specs=[
            pl.BlockSpec((1, slots, tile), lambda c: (c // each, 0, c % each)),
            pl.BlockSpec((tok, slots), lambda c: (0, 0)),
            whole,
            whole,
        ],
        out_specs=(pl.BlockSpec((tok, tile), columns), whole, whole),
        scratch_shapes=[dma((2,))],
        compiler_params=pltpu.CompilerParams(vmem_limit_bytes=56 * 1024 * 1024),
        name="select_rows",
    )(returned.reshape(parts, slots, wide), back, gd, gu)
    return (passed[None], gd.T[None, None], gu[None, None])


def solution(mesh):
    planned = mesh.shape["segment"] == 2 and mesh.shape["owner"] == lines * plane
    return jax.shard_map(
        local_lines if planned else local,
        mesh=mesh,
        in_specs=(
            P("segment", "owner", None),
            P("segment", "owner", None),
            P("owner", None),
            P(),
            P("segment", "owner", None, None),
            P("segment", "owner", None, None),
        ),
        out_specs=(
            P("segment", "owner", None),
            P("segment", "owner", None, None),
            P("segment", "owner", None, None),
        ),
        check_vma=False,
    )
```
